32 devices in a mesh: dp: 4 (over x, core), blk: 2 (over y), mp: 4 (over z).
Axes of the slice: x: 2, y: 2, z: 4, core: 2. Of those that a mesh axis runs over, the one named last changes fastest.
Arguments:
- tokens: bfloat16 [2048, 7168], P('dp', ('blk', 'mp')), may hold values from -6 to 6
- trainer_q: float32 [3584, 7168], P(('mp', 'blk'), 'dp'), may hold values from -0.0625 to 0.0625
- kv_pool: bfloat16 [2, 1024, 3584], P(None, ('dp', 'blk'), 'mp')
- prompt_kv: bfloat16 [2, 2048, 3584], P(None, ('dp', 'blk'), 'mp'), may hold values from -15 to 15
- page_table: int32 [8, 8], P(('dp', 'blk')), may hold values from 0 to 15, as said below
- page_count: int32 [8], P(('dp', 'blk')), may hold values from 1 to 8
- prompt_len: int32 [8], P(('dp', 'blk')), may hold values from 64 to 256
Outputs:
- server_q: bfloat16 [3584, 7168], P('mp', 'blk')
- attn_out: bfloat16 [2048, 3584], P(('dp', 'blk'), 'mp')
The draws below stay inside these ranges and needn't reach their ends.
Inputs may be any that keep to these rules, and one draw needn't show every extreme that they name: `page_table`: the entries of a row are distinct page numbers of the request's group.
All inputs are finite; a program needn't handle non-finite values.
Results may differ from the reference program's by a relative error of at most 0.012.
The reference program's roundings to bfloat16 on the way count: a program that leaves them out, or rounds other values in their place, can miss the bound.
Values may be sent and summed in bfloat16 or wider, within the bound.
No kernel may reach another device: no remote copies, remote signals or barrier semaphores. Data moves between devices by JAX's collectives and lax.ppermute only.
A program may use at most 128 MiB of HBM per device.

```python
import jax
import jax.numpy as jnp
from jax import lax

D = 7168
HEADS = 16
HD = 224
LEN = 256
PAGE = 16
HC = 3584
GROUPS = 4
GROUP_REQS = 2
REQUESTS = 8
TOKENS = 2048
GROUP_PAGES = 16
MAXP = 8
POOL_TOK = 1024


def draw_kv_pool(key, part):
    shape = (2, POOL_TOK, HC)
    values = 2.5 * jax.random.normal(key, shape, jnp.float32)
    return jnp.clip(values, -15.0, 15.0).astype(jnp.bfloat16)


def draw_page_table(key, part):
    row_keys = jax.random.split(key, REQUESTS)

    def one_row(row_key):
        return jax.random.permutation(row_key, GROUP_PAGES)[:MAXP]
    return jax.vmap(one_row)(row_keys).astype(jnp.int32)


def draw_page_count(key, part):
    first_key, second_key, third_key, fourth_key = jax.random.split(key, 4)
    first = jax.random.randint(first_key, (REQUESTS,), 0, MAXP)
    second = jax.random.randint(second_key, (REQUESTS,), 0, MAXP)
    third = jax.random.randint(third_key, (REQUESTS,), 0, MAXP)
    counts = 1 + first * second * third // (MAXP * MAXP)
    fullest = jax.random.randint(fourth_key, (), 0, REQUESTS)
    counts = jnp.where(jnp.arange(REQUESTS) == fullest, MAXP, counts)
    return counts.astype(jnp.int32)


def draw_prompt_len(key, part):
    first_key, second_key = jax.random.split(key)
    lengths = jax.random.randint(first_key, (REQUESTS,), LEN // 4, LEN + 1)
    longest = jax.random.randint(second_key, (), 0, REQUESTS)
    lengths = jnp.where(jnp.arange(REQUESTS) == longest, LEN, lengths)
    return lengths.astype(jnp.int32)


def block_scale(rng, dims, shards, least, high):
    gain, own = 1.0, jax.random.fold_in(rng, 6)
    for axis_at, parts in shards:
        steps = jnp.exp(jax.random.uniform(jax.random.fold_in(own, axis_at), (parts,), jnp.float32, least / len(shards), high / len(shards)))
        gain = gain * jnp.repeat(steps, dims[axis_at] // parts).reshape([-1 if axis == axis_at else 1 for axis in range(len(dims))])
    return gain


def scatter_about(own_key, dims, width, most, shards=(), held_as=jnp.bfloat16):
    drawn = width * jax.random.normal(own_key, dims, jnp.float32)
    if shards:
        drawn = drawn * block_scale(own_key, dims, shards, -0.22, 0.18)
    return jnp.clip(drawn, -most, most).astype(held_as)


def setup_inputs(seed: int = 0) -> dict:
    key_list = jax.random.split(jax.random.key(seed), 8)
    tokens = scatter_about(key_list[0], (TOKENS, D), 1.0, 6.0, ((0, 4), (1, 8)))
    trainer_q = scatter_about(key_list[1], (HC, D), D ** -0.5, 0.0625, ((0, 8), (1, 4)), jnp.float32)
    kv_pool = draw_kv_pool(jax.random.fold_in(key_list[7], 71), 0)
    prompt_kv = scatter_about(key_list[3], (2, TOKENS, HC), 2.5, 15.0, ((1, 8), (2, 4)))
    page_table = draw_page_table(jax.random.fold_in(key_list[7], 71), 0)
    page_count = draw_page_count(jax.random.fold_in(key_list[7], 71), 0)
    prompt_len = draw_prompt_len(jax.random.fold_in(key_list[7], 71), 0)
    return {"tokens": tokens, "trainer_q": trainer_q, "kv_pool": kv_pool, "prompt_kv": prompt_kv, "page_table": page_table, "page_count": page_count, "prompt_len": prompt_len}


very_negative = -1e30


def one_request(request_item, pool_keys, pool_values):
    queries, own_keys, own_values, row_pages, page_total, length, group_index = request_item
    query_heads = queries.reshape(LEN, HEADS, HD).astype(jnp.float32)
    group_keys = lax.dynamic_index_in_dim(pool_keys, group_index, 0, keepdims=False)
    group_values = lax.dynamic_index_in_dim(pool_values, group_index, 0, keepdims=False)
    key_heads = jnp.concatenate([own_keys, group_keys], 0).reshape(-1, HEADS, HD).astype(jnp.float32)
    value_heads = jnp.concatenate([own_values, group_values], 0).reshape(-1, HEADS, HD).astype(jnp.float32)
    page_ids = jnp.arange(GROUP_PAGES * PAGE, dtype=jnp.int32) // PAGE
    live_slots = jnp.arange(MAXP, dtype=jnp.int32) < page_total
    page_used = jnp.any((row_pages[None, :] == page_ids[:, None]) & live_slots[None, :], axis=1)
    row_index = jnp.arange(LEN, dtype=jnp.int32)
    own_mask = (row_index[None, :] <= row_index[:, None]) & (row_index[None, :] < length)
    pool_mask = jnp.broadcast_to(page_used[None, :], (LEN, GROUP_PAGES * PAGE))
    key_mask = jnp.concatenate([own_mask, pool_mask], 1)
    scores = jnp.einsum("thd,khd->htk", query_heads, key_heads) * (HD ** -0.5)
    scores = jnp.where(key_mask[None], scores, very_negative)
    largest = jnp.max(scores, axis=2, keepdims=True)
    weights = jnp.where(key_mask[None], jnp.exp(scores - largest), 0.0)
    row_total = jnp.sum(weights, axis=2)
    rounded = lax.optimization_barrier(weights.astype(jnp.bfloat16)).astype(jnp.float32)
    mixed = jnp.einsum("htk,khd->htd", rounded, value_heads) / row_total[:, :, None]
    mixed = jnp.where((row_index < length)[None, :, None], mixed, 0.0)
    return jnp.transpose(mixed, (1, 0, 2)).reshape(LEN, HEADS * HD).astype(jnp.bfloat16)


def reference(tokens, trainer_q, kv_pool, prompt_kv, page_table, page_count, prompt_len):
    server_q = trainer_q.astype(jnp.bfloat16)
    queries = jnp.dot(tokens, server_q.T, preferred_element_type=jnp.float32).astype(jnp.bfloat16)
    pool_keys = kv_pool[0].reshape(GROUPS, GROUP_PAGES * PAGE, HC)
    pool_values = kv_pool[1].reshape(GROUPS, GROUP_PAGES * PAGE, HC)
    items = (queries.reshape(REQUESTS, LEN, HC),
             prompt_kv[0].reshape(REQUESTS, LEN, HC),
             prompt_kv[1].reshape(REQUESTS, LEN, HC),
             page_table, page_count, prompt_len,
             jnp.arange(REQUESTS, dtype=jnp.int32) // GROUP_REQS)
    mixed = lax.map(lambda request_item: one_request(request_item, pool_keys, pool_values), items)
    return server_q, mixed.reshape(TOKENS, HC)
```

```python
import functools

import jax
import jax.numpy as jnp
from jax import lax
from jax.experimental import pallas as pl
from jax.experimental.pallas import tpu as pltpu
from jax.sharding import PartitionSpec as P

HD = 224
PAGE = 16
AXES = ("dp", "blk", "mp")
BF16 = jnp.bfloat16
F32 = jnp.float32
NT = (((1,), (1,)), ((), ()))


def attend_block(softmax_state, query_heads, key_heads, value_heads, key_mask):
    running_max, row_total, weighted = softmax_state
    scores = jnp.einsum(
        "thd,khd->htk", query_heads, key_heads, preferred_element_type=jnp.float32
    ) * HD ** (-0.5)
    scores = jnp.where(key_mask[None], scores, -1e30)
    new_max = jnp.maximum(running_max, jnp.max(scores, axis=2))
    weights = jnp.where(key_mask[None], jnp.exp(scores - new_max[:, :, None]), 0.0)
    factor = jnp.exp(running_max - new_max)
    row_total = row_total * factor + jnp.sum(weights, axis=2)
    weighted = weighted * factor[:, :, None] + jnp.einsum(
        "htk,khd->htd",
        weights.astype(jnp.bfloat16),
        value_heads,
        preferred_element_type=jnp.float32,
    )
    return (new_max, row_total, weighted)


def body(tokens, trainer_q, kv_pool, prompt_kv, page_table, page_count, prompt_len):
    trainer_rows = lax.all_gather(trainer_q.astype(jnp.bfloat16), "dp", axis=1, tiled=True)
    server_q = lax.all_to_all(trainer_rows, "blk", split_axis=1, concat_axis=0, tiled=True)
    features = lax.all_gather(tokens, "mp", axis=1, tiled=True)
    own_rows = features.shape[0] // lax.axis_size("blk")
    head_width = server_q.shape[0]
    token_local = lax.all_to_all(features, "blk", split_axis=0, concat_axis=1, tiled=True)
    queries = jnp.einsum(
        "td,hd->th",
        token_local,
        lax.all_gather(server_q, "blk", axis=1, tiled=True),
        preferred_element_type=jnp.float32,
    )
    queries = queries.astype(jnp.bfloat16)
    head_count = head_width // HD
    query_heads = queries.reshape(own_rows, head_count, HD)
    length = prompt_len[0]
    row_pages = page_table[0]
    live_slots = jnp.arange(row_pages.shape[0], dtype=jnp.int32) < page_count[0]
    row_index = jnp.arange(own_rows, dtype=jnp.int32)
    own_mask = (row_index[None, :] <= row_index[:, None]) & (row_index[None, :] < length)
    softmax_state = (
        jnp.full((head_count, own_rows), -1e30, jnp.float32),
        jnp.zeros((head_count, own_rows), jnp.float32),
        jnp.zeros((head_count, own_rows, HD), jnp.float32),
    )
    softmax_state = attend_block(
        softmax_state,
        query_heads,
        prompt_kv[0].reshape(own_rows, head_count, HD),
        prompt_kv[1].reshape(own_rows, head_count, HD),
        own_mask,
    )
    shard_piece = lax.all_gather(kv_pool, "blk", axis=1, tiled=True)
    key_count = shard_piece.shape[1]
    page_ids = jnp.arange(key_count, dtype=jnp.int32) // PAGE
    page_used = jnp.any((row_pages[None, :] == page_ids[:, None]) & live_slots[None, :], axis=1)
    key_mask = jnp.broadcast_to(page_used[None, :], (own_rows, key_count))
    running_max, row_total, weighted = attend_block(
        softmax_state,
        query_heads,
        shard_piece[0].reshape(key_count, head_count, HD),
        shard_piece[1].reshape(key_count, head_count, HD),
        key_mask,
    )
    mixed = weighted / row_total[:, :, None]
    mixed = jnp.where((row_index < length)[None, :, None], mixed, 0.0)
    mixed = jnp.transpose(mixed, (1, 0, 2)).reshape(own_rows, head_width).astype(jnp.bfloat16)
    return (server_q, mixed)


def pairs(move):
    def number(pair, core, blk, mp):
        return ((pair * 2 + core) * 2 + blk) * 4 + mp

    found = []
    for pair in range(2):
        for core in range(2):
            for blk in range(2):
                for mp in range(4):
                    target = move(pair, core, blk, mp)
                    if target is not None:
                        found.append((number(pair, core, blk, mp), number(*target)))
    return found


RING = {(0, 0): (1, 0), (1, 0): (1, 1), (1, 1): (0, 1), (0, 1): (0, 0)}
RING_MOVE = pairs(lambda p, c, b, m: (RING[p, b][0], c, RING[p, b][1], m))
CROSS_MOVE = pairs(lambda p, c, b, m: (p, c, b, m) if p == b else (b, c, p, m))
CORE_MOVE = pairs(lambda p, c, b, m: (p, 1 - c, b, m))
BLK_MOVE = pairs(lambda p, c, b, m: (p, c, 1 - b, m))
PAIR_MOVE = pairs(lambda p, c, b, m: (p, c, b, m ^ 1))
MID_MOVE = pairs(lambda p, c, b, m: (p, c, b, 3 - m) if m in (1, 2) else None)
END_MOVE = pairs(lambda p, c, b, m: (p, c, b, m ^ 1) if m in (1, 2) else None)


def place_kernel(where_ref, ring, cross, ring_other, cross_other, out, sems):
    rows, cols = ring.shape
    core, ring_half = where_ref[0], where_ref[1]
    copies = []
    for at, (piece, half, side) in enumerate(
        (
            (ring, ring_half, core),
            (cross, 1 - ring_half, core),
            (ring_other, ring_half, 1 - core),
            (cross_other, 1 - ring_half, 1 - core),
        )
    ):
        target = out.at[
            pl.ds(pl.multiple_of(half * rows, rows), rows),
            pl.ds(pl.multiple_of(side * cols, cols), cols),
        ]
        copies.append(pltpu.make_async_copy(piece, target, sems.at[at]))
    for copy in copies:
        copy.start()
    for copy in copies:
        copy.wait()


def place(where, ring, cross, ring_other, cross_other):
    rows, cols = ring.shape
    any_space = pl.BlockSpec(memory_space=pl.ANY)
    return pl.pallas_call(
        place_kernel,
        out_shape=jax.ShapeDtypeStruct((2 * rows, 2 * cols), BF16),
        in_specs=[pl.BlockSpec(memory_space=pltpu.SMEM)] + [any_space] * 4,
        out_specs=any_space,
        scratch_shapes=[pltpu.SemaphoreType.DMA((4,))],
        cost_estimate=pl.CostEstimate(
            flops=0, bytes_accessed=16 * rows * cols, transcendentals=0
        ),
    )(where, ring, cross, ring_other, cross_other)


def query_kernel(count, final, which, weights, *refs):
    step = pl.program_id(0)
    pieces, rest = refs[: 2 * count], list(refs[2 * count :])
    total = rest.pop()
    before = rest.pop(0) if len(rest) > (2 if final else 1) else None

    @pl.when(step == 0)
    def _():
        total[...] = jnp.zeros_like(total) if before is None else before[...]

    for at in range(count):
        for choice in range(2):

            @pl.when((step == at) & (which[count + at] == choice))
            def _(at=at, choice=choice):
                total[...] += lax.dot_general(
                    pieces[2 * at + choice][...], weights[...], NT, preferred_element_type=F32
                )

    @pl.when(step == count - 1)
    def _():
        if final:
            own, send = rest
            half = own.shape[0]
            blk = which[2 * count]
            own[...] = total[pl.ds(pl.multiple_of(blk * half, half), half), :]
            send[...] = total[
                pl.ds(pl.multiple_of((1 - blk) * half, half), half), :
            ].astype(BF16)
        else:
            rest[0][...] = total[...]


def query_part(which, weights, pieces, before=None, final=True):
    count = len(pieces)
    rows, depth = pieces[0][0].shape
    heads = weights.shape[0]
    flat = [ref for pair in pieces for ref in pair]
    whole = pl.BlockSpec((rows, depth), lambda k, which: (0, 0))
    wide = pl.BlockSpec((rows, heads), lambda k, which: (0, 0))
    in_specs = [pl.BlockSpec((heads, depth), lambda k, which: (0, which[k]))]
    in_specs += [whole] * len(flat)
    operands = [weights] + flat
    if before is not None:
        in_specs.append(wide)
        operands.append(before)
    if final:
        half = pl.BlockSpec((rows // 2, heads), lambda k, which: (0, 0))
        out_specs = [half, half]
        out_shape = [
            jax.ShapeDtypeStruct((rows // 2, heads), F32),
            jax.ShapeDtypeStruct((rows // 2, heads), BF16),
        ]
    else:
        out_specs = wide
        out_shape = jax.ShapeDtypeStruct((rows, heads), F32)
    return pl.pallas_call(
        functools.partial(query_kernel, count, final),
        grid_spec=pltpu.PrefetchScalarGridSpec(
            num_scalar_prefetch=1,
            grid=(count,),
            in_specs=in_specs,
            out_specs=out_specs,
            scratch_shapes=[pltpu.VMEM((rows, heads), F32)],
        ),
        out_shape=out_shape,
        compiler_params=pltpu.CompilerParams(vmem_limit_bytes=40 * 1024 * 1024),
        cost_estimate=pl.CostEstimate(
            flops=2 * count * rows * depth * heads,
            bytes_accessed=2 * count * (rows + heads) * depth,
            transcendentals=0,
        ),
    )(which, *operands)


def attend_kernel(first_row, facts, table, own_q, other_q, prompt, pool_own, pool_other, out, mixed):
    rows, width = out.shape
    heads = width // HD
    length, page_total, blk = facts[0], facts[1], facts[2]
    query = (own_q[...] + other_q[...].astype(F32)).astype(BF16)
    lanes = lax.broadcasted_iota(jnp.int32, (1, width), 1)

    keys_seen = min(prompt.shape[1], -(-(first_row + rows) // 128) * 128)
    row_at = first_row + lax.broadcasted_iota(jnp.int32, (rows, keys_seen), 0)
    key_at = lax.broadcasted_iota(jnp.int32, (rows, keys_seen), 1)
    prompt_bias = jnp.where((key_at <= row_at) & (key_at < length), 0.0, -1e30)

    pool_keys = pool_own.shape[1]

    def pool_bias(side):
        page = side * (pool_keys // PAGE) + (
            lax.broadcasted_iota(jnp.int32, (1, pool_keys), 1) // PAGE
        )
        used = jnp.zeros((1, pool_keys), jnp.int32)
        for slot in range(table.shape[1]):
            hit = (page == table[0, slot]) & (slot < page_total)
            used = jnp.where(hit, 1, used)
        return jnp.where(used > 0, 0.0, -1e30)

    parts = (
        (prompt, keys_seen, prompt_bias),
        (pool_own, pool_keys, pool_bias(blk)),
        (pool_other, pool_keys, pool_bias(1 - blk)),
    )
    live = first_row + lax.broadcasted_iota(jnp.int32, (rows, 1), 0) < length
    for head in range(heads):
        low = head * HD // 128 * 128
        high = min(width, -(-(head + 1) * HD // 128) * 128)
        mine = (lanes >= head * HD) & (lanes < (head + 1) * HD)
        head_q = jnp.where(mine, query, 0)[:, low:high]
        scores = []
        for ref, keys, bias in parts:
            raw = lax.dot_general(
                head_q, ref[0, :keys, low:high], NT, preferred_element_type=F32
            )
            scores.append(jnp.where(bias < 0, -1e30, raw * HD**-0.5))
        largest = functools.reduce(
            jnp.maximum, [jnp.max(s, axis=1, keepdims=True) for s in scores]
        )
        total = 0.0
        value = 0.0
        for (ref, keys, _), score in zip(parts, scores):
            weights = jnp.exp(score - largest)
            total = total + jnp.sum(weights, axis=1, keepdims=True)
            value = value + lax.dot_general(
                weights.astype(BF16),
                ref[1, :keys, low:high],
                (((1,), (0,)), ((), ())),
                preferred_element_type=F32,
            )
        value = jnp.where(live, value / total, 0.0)
        mixed[:, low:high] = jnp.where(mine[:, low:high], value, mixed[:, low:high])
    out[...] = mixed[...].astype(BF16)


def attend(first_row, facts, table, own_q, other_q, prompt, pool_own, pool_other):
    rows, width = own_q.shape
    smem = pl.BlockSpec(memory_space=pltpu.SMEM)
    vmem = pl.BlockSpec(memory_space=pltpu.VMEM)
    return pl.pallas_call(
        functools.partial(attend_kernel, first_row),
        out_shape=jax.ShapeDtypeStruct((rows, width), BF16),
        in_specs=[smem, smem] + [vmem] * 5,
        out_specs=vmem,
        scratch_shapes=[pltpu.VMEM((rows, width), F32)],
        compiler_params=pltpu.CompilerParams(vmem_limit_bytes=40 * 1024 * 1024),
        cost_estimate=pl.CostEstimate(
            flops=4 * rows * 512 * width, bytes_accessed=8 * 512 * width, transcendentals=rows * 2048
        ),
    )(facts, table, own_q, other_q, prompt, pool_own, pool_other)


def square_body(tokens, trainer_q, kv_pool, prompt_kv, page_table, page_count, prompt_len):
    chunks = 2
    dp, blk, mp = (lax.axis_index(name) for name in AXES)
    send = functools.partial(lax.ppermute, axis_name=AXES)
    middle = ((mp == 1) | (mp == 2)).astype(jnp.int32)
    low = (mp < 2).astype(jnp.int32)
    zero = jnp.zeros((), jnp.int32)

    rows = tokens.shape[0]
    by_request = tokens.reshape(2, chunks, rows // (2 * chunks), tokens.shape[1])
    own = [by_request[:, c].reshape(rows // chunks, -1) for c in range(chunks)]
    near = [send(piece, perm=PAIR_MOVE) for piece in own]
    mid_own = [send(piece, perm=MID_MOVE) for piece in own]
    end_own = [send(piece, perm=END_MOVE) for piece in mid_own]
    mid_near = [send(piece, perm=MID_MOVE) for piece in near]
    end_near = [send(piece, perm=END_MOVE) for piece in mid_near]

    own_w = trainer_q.astype(BF16)
    ring = send(own_w, perm=RING_MOVE)
    cross = send(own_w, perm=CROSS_MOVE)
    ring_other = send(ring, perm=CORE_MOVE)
    cross_other = send(cross, perm=CORE_MOVE)
    where = jnp.stack([dp % 2, 1 - dp // 2]).astype(jnp.int32)
    server_q = place(where, ring, cross, ring_other, cross_other)

    pool, _ = lax.optimization_barrier((kv_pool, ring))
    pool_other = send(pool, perm=BLK_MOVE)

    third = jnp.where(low == 1, 2, 1)
    last = jnp.where(low == 1, 3, 0)
    blocks = (mp, mp ^ 1, third, last)
    picks = (zero, zero, 1 - middle, 1 - middle)

    def which(ids):
        return jnp.stack(
            [blocks[i] for i in ids] + [picks[i] for i in ids] + [blk]
        ).astype(jnp.int32)

    facts = jnp.stack([prompt_len[0], page_count[0], blk]).astype(jnp.int32)
    outs = []
    for c in range(chunks):
        pieces = (
            (own[c], own[c]),
            (near[c], near[c]),
            (mid_own[c], end_own[c]),
            (mid_near[c], end_near[c]),
        )
        if c < chunks - 1:
            own_q, send_q = query_part(which((0, 1, 2, 3)), server_q, pieces)
        else:
            early = query_part(which((0, 1, 2)), server_q, pieces[:3], final=False)
            own_q, send_q = query_part(which((3,)), server_q, pieces[3:], before=early)
        other_q = send(send_q, perm=BLK_MOVE)
        outs.append(
            attend(
                c * own_q.shape[0], facts, page_table, own_q, other_q, prompt_kv, kv_pool, pool_other
            )
        )
    return (server_q, jnp.concatenate(outs, axis=0))


def solution(mesh):
    in_specs = (
        P("dp", ("blk", "mp")),
        P(("mp", "blk"), "dp"),
        P(None, ("dp", "blk"), "mp"),
        P(None, ("dp", "blk"), "mp"),
        P(("dp", "blk"), None),
        P(("dp", "blk")),
        P(("dp", "blk")),
    )
    out_specs = (P("mp", "blk"), P(("dp", "blk"), "mp"))
    square = dict(mesh.shape) == {"dp": 4, "blk": 2, "mp": 4}
    return jax.shard_map(
        square_body if square else body,
        mesh=mesh,
        in_specs=in_specs,
        out_specs=out_specs,
        check_vma=False,
    )
```

```python
import functools

import jax
import jax.numpy as jnp
from jax import lax
from jax.experimental import pallas as pl
from jax.experimental.pallas import tpu as pltpu
from jax.sharding import PartitionSpec as P

HD = 224
PAGE = 16
AXES = ("dp", "blk", "mp")
BF16 = jnp.bfloat16
F32 = jnp.float32
NT = (((1,), (1,)), ((), ()))


def attend_block(softmax_state, query_heads, key_heads, value_heads, key_mask):
    running_max, row_total, weighted = softmax_state
    scores = jnp.einsum(
        "thd,khd->htk", query_heads, key_heads, preferred_element_type=jnp.float32
    ) * HD ** (-0.5)
    scores = jnp.where(key_mask[None], scores, -1e30)
    new_max = jnp.maximum(running_max, jnp.max(scores, axis=2))
    weights = jnp.where(key_mask[None], jnp.exp(scores - new_max[:, :, None]), 0.0)
    factor = jnp.exp(running_max - new_max)
    row_total = row_total * factor + jnp.sum(weights, axis=2)
    weighted = weighted * factor[:, :, None] + jnp.einsum(
        "htk,khd->htd",
        weights.astype(jnp.bfloat16),
        value_heads,
        preferred_element_type=jnp.float32,
    )
    return (new_max, row_total, weighted)


def body(tokens, trainer_q, kv_pool, prompt_kv, page_table, page_count, prompt_len):
    trainer_rows = lax.all_gather(trainer_q.astype(jnp.bfloat16), "dp", axis=1, tiled=True)
    server_q = lax.all_to_all(trainer_rows, "blk", split_axis=1, concat_axis=0, tiled=True)
    features = lax.all_gather(tokens, "mp", axis=1, tiled=True)
    own_rows = features.shape[0] // lax.axis_size("blk")
    head_width = server_q.shape[0]
    token_local = lax.all_to_all(features, "blk", split_axis=0, concat_axis=1, tiled=True)
    queries = jnp.einsum(
        "td,hd->th",
        token_local,
        lax.all_gather(server_q, "blk", axis=1, tiled=True),
        preferred_element_type=jnp.float32,
    )
    queries = queries.astype(jnp.bfloat16)
    head_count = head_width // HD
    query_heads = queries.reshape(own_rows, head_count, HD)
    length = prompt_len[0]
    row_pages = page_table[0]
    live_slots = jnp.arange(row_pages.shape[0], dtype=jnp.int32) < page_count[0]
    row_index = jnp.arange(own_rows, dtype=jnp.int32)
    own_mask = (row_index[None, :] <= row_index[:, None]) & (row_index[None, :] < length)
    softmax_state = (
        jnp.full((head_count, own_rows), -1e30, jnp.float32),
        jnp.zeros((head_count, own_rows), jnp.float32),
        jnp.zeros((head_count, own_rows, HD), jnp.float32),
    )
    softmax_state = attend_block(
        softmax_state,
        query_heads,
        prompt_kv[0].reshape(own_rows, head_count, HD),
        prompt_kv[1].reshape(own_rows, head_count, HD),
        own_mask,
    )
    shard_piece = lax.all_gather(kv_pool, "blk", axis=1, tiled=True)
    key_count = shard_piece.shape[1]
    page_ids = jnp.arange(key_count, dtype=jnp.int32) // PAGE
    page_used = jnp.any((row_pages[None, :] == page_ids[:, None]) & live_slots[None, :], axis=1)
    key_mask = jnp.broadcast_to(page_used[None, :], (own_rows, key_count))
    running_max, row_total, weighted = attend_block(
        softmax_state,
        query_heads,
        shard_piece[0].reshape(key_count, head_count, HD),
        shard_piece[1].reshape(key_count, head_count, HD),
        key_mask,
    )
    mixed = weighted / row_total[:, :, None]
    mixed = jnp.where((row_index < length)[None, :, None], mixed, 0.0)
    mixed = jnp.transpose(mixed, (1, 0, 2)).reshape(own_rows, head_width).astype(jnp.bfloat16)
    return (server_q, mixed)


def pairs(move):
    def number(pair, core, blk, mp):
        return ((pair * 2 + core) * 2 + blk) * 4 + mp

    found = []
    for pair in range(2):
        for core in range(2):
            for blk in range(2):
                for mp in range(4):
                    target = move(pair, core, blk, mp)
                    if target is not None:
                        found.append((number(pair, core, blk, mp), number(*target)))
    return found


RING = {(0, 0): (1, 0), (1, 0): (1, 1), (1, 1): (0, 1), (0, 1): (0, 0)}
RING_MOVE = pairs(lambda p, c, b, m: (RING[p, b][0], c, RING[p, b][1], m))
CROSS_MOVE = pairs(lambda p, c, b, m: (p, c, b, m) if p == b else (b, c, p, m))
CORE_MOVE = pairs(lambda p, c, b, m: (p, 1 - c, b, m))
BLK_MOVE = pairs(lambda p, c, b, m: (p, c, 1 - b, m))
PAIR_MOVE = pairs(lambda p, c, b, m: (p, c, b, m ^ 1))
MID_MOVE = pairs(lambda p, c, b, m: (p, c, b, 3 - m) if m in (1, 2) else None)
END_MOVE = pairs(lambda p, c, b, m: (p, c, b, m ^ 1) if m in (1, 2) else None)


def query_kernel(facts, *refs):
    wide, sides = refs[:4], (refs[4:6], refs[6:8])
    total, last_w, server_q, held_t, held_w, got_t, got_w, put_w = refs[8:]
    middle, ring_half = facts[1], facts[2]
    rows, depth = sides[0][0].shape[0], held_w.shape[2]

    def fetch_t(k, source):
        return pltpu.make_async_copy(wide[k + source], held_t.at[k], got_t.at[k])

    def fetch_w(k, side, source):
        part = ring_half if source == 0 else 1 - ring_half
        return pltpu.make_async_copy(
            sides[side][source].at[
                :, pl.ds(pl.multiple_of(facts[5 + 3 * k] * depth, 128), depth)
            ],
            held_w.at[k, pl.ds(pl.multiple_of(part * rows, 16), rows)],
            got_w.at[k, source],
        )

    def store_w(k):
        return pltpu.make_async_copy(
            held_w.at[k],
            server_q.at[:, pl.ds(pl.multiple_of(facts[3 + 3 * k] * depth, 128), depth)],
            put_w.at[k],
        )

    for k in range(4):
        for side in range(2):

            @pl.when(facts[4 + 3 * k] == side)
            def _(k=k, side=side):
                for source in range(2):
                    fetch_w(k, side, source).start()

        if k < 2:
            fetch_t(k, 0).start()
        elif k == 2:
            for source in range(2):

                @pl.when(middle == 1 - source)
                def _(k=k, source=source):
                    fetch_t(k, source).start()

    for k in range(4):
        for source in range(2):
            fetch_w(k, 0, source).wait()
        store_w(k).start()
        if k == 3:
            last_w[...] = held_w[k]
        else:
            fetch_t(k, 0).wait()
            part = lax.dot_general(held_t[k], held_w[k], NT, preferred_element_type=F32)
            if k == 0:
                total[...] = part
            else:
                total[...] += part
    for k in range(4):
        store_w(k).wait()


def query_part(facts, wide, sides):
    rows, depth = wide[0].shape
    heads = 2 * sides[0].shape[0]
    vmem = pl.BlockSpec(memory_space=pltpu.VMEM)
    anywhere = pl.BlockSpec(memory_space=pl.ANY)
    return pl.pallas_call(
        query_kernel,
        out_shape=(
            jax.ShapeDtypeStruct((rows, heads), F32),
            jax.ShapeDtypeStruct((heads, depth), BF16),
            jax.ShapeDtypeStruct((heads, 4 * depth), BF16),
        ),
        in_specs=[pl.BlockSpec(memory_space=pltpu.SMEM)] + [anywhere] * 8,
        out_specs=(vmem, vmem, anywhere),
        scratch_shapes=[
            pltpu.VMEM((3, rows, depth), BF16),
            pltpu.VMEM((4, heads, depth), BF16),
            pltpu.SemaphoreType.DMA((3,)),
            pltpu.SemaphoreType.DMA((4, 2)),
            pltpu.SemaphoreType.DMA((4,)),
        ],
        compiler_params=pltpu.CompilerParams(vmem_limit_bytes=40 * 1024 * 1024),
        cost_estimate=pl.CostEstimate(
            flops=2 * 3 * rows * depth * heads,
            bytes_accessed=2 * 4 * (rows + 2 * heads) * depth,
            transcendentals=0,
        ),
    )(facts, *wide, *sides)


def last_kernel(chunk, facts, mid_piece, end_piece, so_far, weights, own, send, held_t, held_s, got):
    middle, blk = facts[1], facts[0]
    half = own.shape[0]
    for source, piece in enumerate((mid_piece, end_piece)):

        @pl.when(middle == 1 - source)
        def _(piece=piece):
            pltpu.make_async_copy(piece, held_t, got.at[0]).start()

    sums = [
        pltpu.make_async_copy(
            so_far.at[pl.ds((2 * request + chunk) * half, half)],
            held_s.at[request],
            got.at[1 + request],
        )
        for request in range(2)
    ]
    for copy in sums:
        copy.start()
    pltpu.make_async_copy(mid_piece, held_t, got.at[0]).wait()
    part = lax.dot_general(held_t[...], weights[...], NT, preferred_element_type=F32)
    for copy in sums:
        copy.wait()
    upper, lower = held_s[0] + part[:half], held_s[1] + part[half:]

    @pl.when(blk == 0)
    def _():
        own[...] = upper
        send[...] = lower.astype(BF16)

    @pl.when(blk == 1)
    def _():
        own[...] = lower
        send[...] = upper.astype(BF16)


def query_last(chunk, facts, mid_piece, end_piece, so_far, weights):
    rows, depth = mid_piece.shape
    heads = weights.shape[0]
    vmem = pl.BlockSpec(memory_space=pltpu.VMEM)
    anywhere = pl.BlockSpec(memory_space=pl.ANY)
    return pl.pallas_call(
        functools.partial(last_kernel, chunk),
        out_shape=(
            jax.ShapeDtypeStruct((rows // 2, heads), F32),
            jax.ShapeDtypeStruct((rows // 2, heads), BF16),
        ),
        in_specs=[pl.BlockSpec(memory_space=pltpu.SMEM)] + [anywhere] * 3 + [vmem],
        out_specs=(vmem,) * 2,
        scratch_shapes=[
            pltpu.VMEM((rows, depth), BF16),
            pltpu.VMEM((2, rows // 2, heads), F32),
            pltpu.SemaphoreType.DMA((3,)),
        ],
        compiler_params=pltpu.CompilerParams(vmem_limit_bytes=40 * 1024 * 1024),
        cost_estimate=pl.CostEstimate(
            flops=2 * rows * depth * heads,
            bytes_accessed=2 * (2 * rows + heads) * depth,
            transcendentals=0,
        ),
    )(facts, mid_piece, end_piece, so_far, weights)


def attend_kernel(first_row, facts, table, own_q, other_q, prompt, pool_own, pool_other, *refs):
    out, mixed = refs[-2:]
    rows, width = out.shape
    heads = width // HD
    length, page_total, blk = facts[0], facts[1], facts[2]
    query = (own_q[...] + other_q[...].astype(F32)).astype(BF16)
    lanes = lax.broadcasted_iota(jnp.int32, (1, width), 1)

    keys_seen = min(prompt.shape[1], -(-(first_row + rows) // 128) * 128)
    row_at = first_row + lax.broadcasted_iota(jnp.int32, (rows, keys_seen), 0)
    key_at = lax.broadcasted_iota(jnp.int32, (rows, keys_seen), 1)
    prompt_bias = jnp.where((key_at <= row_at) & (key_at < length), 0.0, -1e30)

    pool_keys = pool_own.shape[1]

    def pool_bias(side):
        page = side * (pool_keys // PAGE) + (
            lax.broadcasted_iota(jnp.int32, (1, pool_keys), 1) // PAGE
        )
        used = jnp.zeros((1, pool_keys), jnp.int32)
        for slot in range(table.shape[1]):
            hit = (page == table[0, slot]) & (slot < page_total)
            used = jnp.where(hit, 1, used)
        return jnp.where(used > 0, 0.0, -1e30)

    parts = (
        (prompt, keys_seen, prompt_bias),
        (pool_own, pool_keys, pool_bias(blk)),
        (pool_other, pool_keys, pool_bias(1 - blk)),
    )
    live = first_row + lax.broadcasted_iota(jnp.int32, (rows, 1), 0) < length
    for head in range(heads):
        low = head * HD // 128 * 128
        high = min(width, -(-(head + 1) * HD // 128) * 128)
        mine = (lanes >= head * HD) & (lanes < (head + 1) * HD)
        head_q = jnp.where(mine, query, 0)[:, low:high]
        scores = []
        for ref, keys, bias in parts:
            raw = lax.dot_general(
                head_q, ref[0, :keys, low:high], NT, preferred_element_type=F32
            )
            scores.append(jnp.where(bias < 0, -1e30, raw * HD**-0.5))
        largest = functools.reduce(
            jnp.maximum, [jnp.max(s, axis=1, keepdims=True) for s in scores]
        )
        total = 0.0
        value = 0.0
        for (ref, keys, _), score in zip(parts, scores):
            weights = jnp.exp(score - largest)
            total = total + jnp.sum(weights, axis=1, keepdims=True)
            value = value + lax.dot_general(
                weights.astype(BF16),
                ref[1, :keys, low:high],
                (((1,), (0,)), ((), ())),
                preferred_element_type=F32,
            )
        value = jnp.where(live, value / total, 0.0)
        mixed[:, low:high] = jnp.where(mine[:, low:high], value, mixed[:, low:high])
    out[...] = mixed[...].astype(BF16)


def attend(first_row, facts, table, own_q, other_q, prompt, pool_own, pool_other, before=None):
    rows, width = own_q.shape
    all_rows = prompt.shape[1]
    smem = pl.BlockSpec(memory_space=pltpu.SMEM)
    vmem = pl.BlockSpec(memory_space=pltpu.VMEM)
    in_specs = [smem, smem] + [vmem] * 5
    operands = [facts, table, own_q, other_q, prompt, pool_own, pool_other]
    if before is not None:
        in_specs.append(pl.BlockSpec(memory_space=pl.ANY))
        operands.append(before)
    return pl.pallas_call(
        functools.partial(attend_kernel, first_row),
        grid=(1,),
        out_shape=jax.ShapeDtypeStruct((all_rows, width), BF16),
        in_specs=in_specs,
        out_specs=pl.BlockSpec((rows, width), lambda i: (first_row // rows, 0)),
        scratch_shapes=[pltpu.VMEM((rows, width), F32)],
        input_output_aliases={} if before is None else {7: 0},
        compiler_params=pltpu.CompilerParams(vmem_limit_bytes=40 * 1024 * 1024),
        cost_estimate=pl.CostEstimate(
            flops=4 * rows * 512 * width, bytes_accessed=8 * 512 * width, transcendentals=rows * 2048
        ),
    )(*operands)


def square_body(tokens, trainer_q, kv_pool, prompt_kv, page_table, page_count, prompt_len):
    dp, blk, mp = (lax.axis_index(name) for name in AXES)
    core, ring_half = dp % 2, 1 - dp // 2
    send = functools.partial(lax.ppermute, axis_name=AXES)

    near = send(tokens, perm=PAIR_MOVE)
    mid_own = send(tokens, perm=MID_MOVE)
    end_own = send(mid_own, perm=END_MOVE)
    by_request = near.reshape(2, 2, near.shape[0] // 4, near.shape[1])
    mid_near = [
        send(by_request[:, c].reshape(-1, near.shape[1]), perm=MID_MOVE) for c in range(2)
    ]
    end_near = [send(piece, perm=END_MOVE) for piece in mid_near]

    own_w = trainer_q.astype(BF16)
    ring = send(own_w, perm=RING_MOVE)
    cross = send(own_w, perm=CROSS_MOVE)
    ring, cross, pool, _ = lax.optimization_barrier(
        (ring, cross, kv_pool, (end_own, mid_near[0]))
    )
    ring_other = send(ring, perm=CORE_MOVE)
    cross_other = send(cross, perm=CORE_MOVE)
    pool_other = send(pool, perm=BLK_MOVE)

    third = jnp.where(mp < 2, 2, 1)
    last = jnp.where(mp < 2, 3, 0)
    middle = (mp == 1) | (mp == 2)
    facts = [blk, middle, ring_half]
    for place_at in (mp, mp ^ 1, third, last):
        facts += [place_at, place_at // 2 != core, place_at % 2]
    facts = jnp.stack([jnp.asarray(f, jnp.int32) for f in facts])
    so_far, last_w, server_q = query_part(
        facts, (tokens, near, mid_own, end_own), (ring, cross, ring_other, cross_other)
    )
    own_q, send_q = zip(
        *(query_last(c, facts, mid_near[c], end_near[c], so_far, last_w) for c in range(2))
    )
    other_q = [send(piece, perm=BLK_MOVE) for piece in send_q]

    live = jnp.stack([prompt_len[0], page_count[0], blk]).astype(jnp.int32)
    out = None
    for c in range(2):
        out = attend(
            c * own_q[c].shape[0],
            live,
            page_table,
            own_q[c],
            other_q[c],
            prompt_kv,
            kv_pool,
            pool_other,
            out,
        )
    return (server_q, out)


def solution(mesh):
    in_specs = (
        P("dp", ("blk", "mp")),
        P(("mp", "blk"), "dp"),
        P(None, ("dp", "blk"), "mp"),
        P(None, ("dp", "blk"), "mp"),
        P(("dp", "blk"), None),
        P(("dp", "blk")),
        P(("dp", "blk")),
    )
    out_specs = (P("mp", "blk"), P(("dp", "blk"), "mp"))
    square = dict(mesh.shape) == {"dp": 4, "blk": 2, "mp": 4}
    return jax.shard_map(
        square_body if square else body,
        mesh=mesh,
        in_specs=in_specs,
        out_specs=out_specs,
        check_vma=False,
    )
```

```python
import functools

import jax
import jax.numpy as jnp
from jax import lax
from jax.experimental import pallas as pl
from jax.experimental.pallas import tpu as pltpu
from jax.sharding import PartitionSpec as P

HD = 224
PAGE = 16
W_PARTS = 1
CUT = 160
AXES = ("dp", "blk", "mp")
BF16 = jnp.bfloat16
F32 = jnp.float32
NT = (((1,), (1,)), ((), ()))


def attend_block(softmax_state, query_heads, key_heads, value_heads, key_mask):
    running_max, row_total, weighted = softmax_state
    scores = jnp.einsum(
        "thd,khd->htk", query_heads, key_heads, preferred_element_type=jnp.float32
    ) * HD ** (-0.5)
    scores = jnp.where(key_mask[None], scores, -1e30)
    new_max = jnp.maximum(running_max, jnp.max(scores, axis=2))
    weights = jnp.where(key_mask[None], jnp.exp(scores - new_max[:, :, None]), 0.0)
    factor = jnp.exp(running_max - new_max)
    row_total = row_total * factor + jnp.sum(weights, axis=2)
    weighted = weighted * factor[:, :, None] + jnp.einsum(
        "htk,khd->htd",
        weights.astype(jnp.bfloat16),
        value_heads,
        preferred_element_type=jnp.float32,
    )
    return (new_max, row_total, weighted)


def body(tokens, trainer_q, kv_pool, prompt_kv, page_table, page_count, prompt_len):
    trainer_rows = lax.all_gather(trainer_q.astype(jnp.bfloat16), "dp", axis=1, tiled=True)
    server_q = lax.all_to_all(trainer_rows, "blk", split_axis=1, concat_axis=0, tiled=True)
    features = lax.all_gather(tokens, "mp", axis=1, tiled=True)
    own_rows = features.shape[0] // lax.axis_size("blk")
    head_width = server_q.shape[0]
    token_local = lax.all_to_all(features, "blk", split_axis=0, concat_axis=1, tiled=True)
    queries = jnp.einsum(
        "td,hd->th",
        token_local,
        lax.all_gather(server_q, "blk", axis=1, tiled=True),
        preferred_element_type=jnp.float32,
    )
    queries = queries.astype(jnp.bfloat16)
    head_count = head_width // HD
    query_heads = queries.reshape(own_rows, head_count, HD)
    length = prompt_len[0]
    row_pages = page_table[0]
    live_slots = jnp.arange(row_pages.shape[0], dtype=jnp.int32) < page_count[0]
    row_index = jnp.arange(own_rows, dtype=jnp.int32)
    own_mask = (row_index[None, :] <= row_index[:, None]) & (row_index[None, :] < length)
    softmax_state = (
        jnp.full((head_count, own_rows), -1e30, jnp.float32),
        jnp.zeros((head_count, own_rows), jnp.float32),
        jnp.zeros((head_count, own_rows, HD), jnp.float32),
    )
    softmax_state = attend_block(
        softmax_state,
        query_heads,
        prompt_kv[0].reshape(own_rows, head_count, HD),
        prompt_kv[1].reshape(own_rows, head_count, HD),
        own_mask,
    )
    shard_piece = lax.all_gather(kv_pool, "blk", axis=1, tiled=True)
    key_count = shard_piece.shape[1]
    page_ids = jnp.arange(key_count, dtype=jnp.int32) // PAGE
    page_used = jnp.any((row_pages[None, :] == page_ids[:, None]) & live_slots[None, :], axis=1)
    key_mask = jnp.broadcast_to(page_used[None, :], (own_rows, key_count))
    running_max, row_total, weighted = attend_block(
        softmax_state,
        query_heads,
        shard_piece[0].reshape(key_count, head_count, HD),
        shard_piece[1].reshape(key_count, head_count, HD),
        key_mask,
    )
    mixed = weighted / row_total[:, :, None]
    mixed = jnp.where((row_index < length)[None, :, None], mixed, 0.0)
    mixed = jnp.transpose(mixed, (1, 0, 2)).reshape(own_rows, head_width).astype(jnp.bfloat16)
    return (server_q, mixed)


def pairs(move):
    def number(pair, core, blk, mp):
        return ((pair * 2 + core) * 2 + blk) * 4 + mp

    found = []
    for pair in range(2):
        for core in range(2):
            for blk in range(2):
                for mp in range(4):
                    target = move(pair, core, blk, mp)
                    if target is not None:
                        found.append((number(pair, core, blk, mp), number(*target)))
    return found


RING = {(0, 0): (1, 0), (1, 0): (1, 1), (1, 1): (0, 1), (0, 1): (0, 0)}
RING_MOVE = pairs(lambda p, c, b, m: (RING[p, b][0], c, RING[p, b][1], m))
CROSS_MOVE = pairs(lambda p, c, b, m: (p, c, b, m) if p == b else (b, c, p, m))
CORE_MOVE = pairs(lambda p, c, b, m: (p, 1 - c, b, m))
BLK_MOVE = pairs(lambda p, c, b, m: (p, c, 1 - b, m))
PAIR_MOVE = pairs(lambda p, c, b, m: (p, c, b, m ^ 1))
MID_MOVE = pairs(lambda p, c, b, m: (p, c, b, 3 - m) if m in (1, 2) else None)
END_MOVE = pairs(lambda p, c, b, m: (p, c, b, m ^ 1) if m in (1, 2) else None)


def cut_kernel(piece, *parts):
    half = piece.shape[0] // 2
    row = 0
    for part in parts:
        rows = part.shape[0] // 2
        for request in range(2):
            part[request * rows : (request + 1) * rows] = piece[
                request * half + row : request * half + row + rows
            ]
        row += rows


def cut(piece, first):
    rows, depth = piece.shape
    vmem = pl.BlockSpec(memory_space=pltpu.VMEM)
    return pl.pallas_call(
        cut_kernel,
        out_shape=(
            pltpu.VMEM((2 * first, depth), piece.dtype),
            pltpu.VMEM((rows - 2 * first, depth), piece.dtype),
        ),
        in_specs=[vmem],
        out_specs=(vmem, vmem),
        compiler_params=pltpu.CompilerParams(vmem_limit_bytes=8 * 1024 * 1024),
        cost_estimate=pl.CostEstimate(
            flops=0, bytes_accessed=4 * rows * depth, transcendentals=0
        ),
    )(piece)


def query_kernel(facts, *refs):
    wide = refs[:4]
    sides = (refs[4 : 4 + 2 * W_PARTS], refs[4 + 2 * W_PARTS : 4 + 4 * W_PARTS])
    total, last_w, server_q, held_t, held_w, got_t, got_w, put_w = refs[4 + 4 * W_PARTS + 1 :]
    middle, ring_half = facts[1], facts[2]
    rows, depth = sides[0][0].shape[0], held_w.shape[2]

    def fetch_t(k, source):
        return pltpu.make_async_copy(wide[k + source], held_t.at[k], got_t.at[k])

    def fetch_w(k, side, source):
        part = ring_half if source < W_PARTS else 1 - ring_half
        first_row = (part * W_PARTS + source % W_PARTS) * rows
        return pltpu.make_async_copy(
            sides[side][source].at[
                :, pl.ds(pl.multiple_of(facts[5 + 3 * k] * depth, 128), depth)
            ],
            held_w.at[k, pl.ds(pl.multiple_of(first_row, 16), rows)],
            got_w.at[k, source],
        )

    def store_w(k):
        return pltpu.make_async_copy(
            held_w.at[k],
            server_q.at[:, pl.ds(pl.multiple_of(facts[3 + 3 * k] * depth, 128), depth)],
            put_w.at[k],
        )

    for k in range(4):
        for side in range(2):

            @pl.when(facts[4 + 3 * k] == side)
            def _(k=k, side=side):
                for source in range(2 * W_PARTS):
                    fetch_w(k, side, source).start()

        if k < 2:
            fetch_t(k, 0).start()
        elif k == 2:
            for source in range(2):

                @pl.when(middle == 1 - source)
                def _(k=k, source=source):
                    fetch_t(k, source).start()

    for k in range(4):
        for source in range(2 * W_PARTS):
            fetch_w(k, 0, source).wait()
        store_w(k).start()
        if k == 3:
            last_w[...] = held_w[k]
        else:
            fetch_t(k, 0).wait()
            part = lax.dot_general(held_t[k], held_w[k], NT, preferred_element_type=F32)
            if k == 0:
                total[...] = part
            else:
                total[...] += part
    for k in range(4):
        store_w(k).wait()


def query_part(facts, wide, sides, token):
    rows, depth = wide[0].shape
    heads = 2 * W_PARTS * sides[0].shape[0]
    in_hbm = functools.partial(pltpu.with_memory_space_constraint, memory_space=pltpu.HBM)
    wide = [in_hbm(piece) for piece in wide]
    sides = [in_hbm(piece) for piece in sides]
    vmem = pl.BlockSpec(memory_space=pltpu.VMEM)
    anywhere = pl.BlockSpec(memory_space=pl.ANY)
    return pl.pallas_call(
        query_kernel,
        out_shape=(
            pltpu.VMEM((rows, heads), F32),
            pltpu.VMEM((heads, depth), BF16),
            jax.ShapeDtypeStruct((heads, 4 * depth), BF16),
        ),
        in_specs=[pl.BlockSpec(memory_space=pltpu.SMEM)] + [anywhere] * (4 + 4 * W_PARTS + 1),
        out_specs=(vmem, vmem, anywhere),
        scratch_shapes=[
            pltpu.VMEM((3, rows, depth), BF16),
            pltpu.VMEM((4, heads, depth), BF16),
            pltpu.SemaphoreType.DMA((3,)),
            pltpu.SemaphoreType.DMA((4, 2 * W_PARTS)),
            pltpu.SemaphoreType.DMA((4,)),
        ],
        compiler_params=pltpu.CompilerParams(vmem_limit_bytes=14 * 1024 * 1024),
        cost_estimate=pl.CostEstimate(
            flops=2 * 3 * rows * depth * heads,
            bytes_accessed=2 * 4 * (rows + 2 * heads) * depth,
            transcendentals=0,
        ),
    )(facts, *wide, *sides, *token)


def last_kernel(first_row, facts, mid_piece, end_piece, so_far, weights, own, send):
    middle, blk = facts[1], facts[0]
    half = own.shape[0]
    piece = jnp.where(middle == 1, mid_piece[...], end_piece[...])
    part = lax.dot_general(piece, weights[...], NT, preferred_element_type=F32)
    whole = so_far.shape[0] // 2
    upper = so_far[first_row : first_row + half] + part[:half]
    lower = so_far[whole + first_row : whole + first_row + half] + part[half:]

    @pl.when(blk == 0)
    def _():
        own[...] = upper
        send[...] = lower.astype(BF16)

    @pl.when(blk == 1)
    def _():
        own[...] = lower
        send[...] = upper.astype(BF16)


def query_last(first_row, facts, mid_piece, end_piece, so_far, weights):
    rows, depth = mid_piece.shape
    heads = weights.shape[0]
    vmem = pl.BlockSpec(memory_space=pltpu.VMEM)
    return pl.pallas_call(
        functools.partial(last_kernel, first_row),
        out_shape=(
            jax.ShapeDtypeStruct((rows // 2, heads), F32),
            jax.ShapeDtypeStruct((rows // 2, heads), BF16),
        ),
        in_specs=[pl.BlockSpec(memory_space=pltpu.SMEM)] + [vmem] * 4,
        out_specs=(vmem,) * 2,
        compiler_params=pltpu.CompilerParams(vmem_limit_bytes=6 * 1024 * 1024),
        cost_estimate=pl.CostEstimate(
            flops=2 * rows * depth * heads,
            bytes_accessed=2 * (2 * rows + heads) * depth,
            transcendentals=0,
        ),
    )(facts, mid_piece, end_piece, so_far, weights)


def window(head, width):
    low = head * HD // 128 * 128
    high = min(width, -(-(head + 1) * HD // 128) * 128)
    return low, high, head * HD - low


def to_front(wide, offset):
    if offset:
        wide = pltpu.roll(wide, wide.shape[1] - offset, 1)
    return wide[:, :256]


def align_kernel(prompt, pool_own, pool_other, out):
    width = prompt.shape[2]
    for kind in range(2):
        row = 0
        for ref in (pool_own, pool_other, prompt):
            rows = ref.shape[1]
            for head in range(width // HD):
                low, high, offset = window(head, width)
                wide = ref[kind, :, low:high].astype(F32)
                out[kind, head, row : row + rows] = to_front(wide, offset).astype(BF16)
            row += rows


def align(prompt, pool_own, pool_other):
    width = prompt.shape[2]
    keys = prompt.shape[1] + pool_own.shape[1] + pool_other.shape[1]
    vmem = pl.BlockSpec(memory_space=pltpu.VMEM)
    return pl.pallas_call(
        align_kernel,
        out_shape=jax.ShapeDtypeStruct((2, width // HD, keys, 256), BF16),
        in_specs=[vmem] * 3,
        out_specs=vmem,
        compiler_params=pltpu.CompilerParams(vmem_limit_bytes=12 * 1024 * 1024),
        cost_estimate=pl.CostEstimate(
            flops=0, bytes_accessed=8 * keys * width, transcendentals=0
        ),
    )(prompt, pool_own, pool_other)


def attend_kernel(first_row, pool_keys, facts, own_q, other_q, aligned, *refs):
    out, done, sem = refs[-3:]
    rows, width = done.shape
    heads = width // HD
    length, page_total, blk = facts[15], facts[16], facts[0]
    query = (own_q[...] + other_q[...].astype(F32)).astype(BF16).astype(F32)

    keys = 2 * pool_keys + first_row + rows
    key_at = lax.broadcasted_iota(jnp.int32, (1, keys), 1)
    own_side = key_at < pool_keys
    pages_here = pool_keys // PAGE
    page = jnp.where(own_side, blk, -blk) * pages_here + key_at // PAGE
    used = jnp.zeros((1, keys), jnp.int32)
    for slot in range(facts.shape[0] - 17):
        used = jnp.where((page == facts[17 + slot]) & (slot < page_total), 1, used)
    prompt_at = key_at - 2 * pool_keys
    seen_from = jnp.where(
        prompt_at >= 0,
        jnp.where(prompt_at < length, prompt_at, first_row + rows),
        jnp.where(used > 0, 0, first_row + rows),
    )
    row_at = first_row + lax.broadcasted_iota(jnp.int32, (rows, 1), 0)
    seen = seen_from <= row_at
    live = row_at < length
    lanes = lax.broadcasted_iota(jnp.int32, (1, 256), 1)

    raw = []
    for head in range(heads):
        low, high, offset = window(head, width)
        head_q = jnp.where(lanes < HD, to_front(query[:, low:high], offset), 0.0).astype(BF16)
        raw.append(
            lax.dot_general(head_q, aligned[0, head, :keys], NT, preferred_element_type=F32)
        )
    tiles = [None] * (width // 128)
    for head in range(heads):
        low, high, offset = window(head, width)
        scores = jnp.where(seen, raw[head] * HD**-0.5, -1e30)
        weights = jnp.exp(scores - jnp.max(scores, axis=1, keepdims=True))
        total = jnp.sum(weights, axis=1, keepdims=True)
        value = jnp.dot(
            weights.astype(BF16), aligned[1, head, :keys], preferred_element_type=F32
        )
        value = jnp.where(live, value * (1.0 / total), 0.0)
        if high - low > 256:
            value = jnp.concatenate([value, jnp.zeros((rows, high - low - 256), F32)], axis=1)
        if offset:
            value = pltpu.roll(value, offset, 1)
        for tile in range(low // 128, high // 128):
            part = value[:, tile * 128 - low : (tile + 1) * 128 - low]
            if tiles[tile] is None:
                tiles[tile] = part
            else:
                tiles[tile] = jnp.where(
                    lanes[:, :128] < head * HD - tile * 128, tiles[tile], part
                )
    for tile, part in enumerate(tiles):
        done[:, tile * 128 : (tile + 1) * 128] = part.astype(BF16)
    copy = pltpu.make_async_copy(done, out.at[pl.ds(first_row, rows)], sem)
    copy.start()
    copy.wait()


def attend(first_row, pool_keys, facts, own_q, other_q, aligned, before=None):
    rows, width = own_q.shape
    all_rows = aligned.shape[2] - 2 * pool_keys
    smem = pl.BlockSpec(memory_space=pltpu.SMEM)
    vmem = pl.BlockSpec(memory_space=pltpu.VMEM)
    in_specs = [smem] + [vmem] * 3
    operands = [facts, own_q, other_q, aligned]
    if before is not None:
        in_specs.append(pl.BlockSpec(memory_space=pl.ANY))
        operands.append(before)
    return pl.pallas_call(
        functools.partial(attend_kernel, first_row, pool_keys),
        out_shape=jax.ShapeDtypeStruct((all_rows, width), BF16),
        in_specs=in_specs,
        out_specs=pl.BlockSpec(memory_space=pl.ANY),
        scratch_shapes=[
            pltpu.VMEM((rows, width), BF16),
            pltpu.SemaphoreType.DMA(()),
        ],
        input_output_aliases={} if before is None else {4: 0},
        compiler_params=pltpu.CompilerParams(vmem_limit_bytes=8 * 1024 * 1024),
        cost_estimate=pl.CostEstimate(
            flops=4 * rows * 512 * width, bytes_accessed=8 * 512 * width, transcendentals=rows * 2048
        ),
    )(*operands)


def square_body(tokens, trainer_q, kv_pool, prompt_kv, page_table, page_count, prompt_len):
    dp, blk, mp = (lax.axis_index(name) for name in AXES)
    core, ring_half = dp % 2, 1 - dp // 2
    send = functools.partial(lax.ppermute, axis_name=AXES)

    near = send(tokens, perm=PAIR_MOVE)
    mid_own = send(tokens, perm=MID_MOVE)
    end_own = send(mid_own, perm=END_MOVE)
    parts = cut(near, CUT)
    mid_near = [send(parts[0], perm=MID_MOVE)]
    mid_near.append(send(parts[1], perm=MID_MOVE))
    end_near = [send(piece, perm=END_MOVE) for piece in mid_near]

    token = []
    late = []
    piece = near[:256]
    for _ in range(1):
        piece = send(piece, perm=CORE_MOVE)
    token.append(piece)
    rows = trainer_q.shape[0] // W_PARTS
    own_w = [trainer_q[p * rows : (p + 1) * rows].astype(BF16) for p in range(W_PARTS)]
    ring = [send(piece, perm=RING_MOVE) for piece in own_w]
    cross = [send(piece, perm=CROSS_MOVE) for piece in own_w]
    ring, cross, token, _ = lax.optimization_barrier((ring, cross, token, (end_own, mid_near[0], mid_near[1], )))
    pool = kv_pool
    pool, _ = lax.optimization_barrier((kv_pool, (ring,)))
    ring_other = [send(piece, perm=CORE_MOVE) for piece in ring]
    cross_other = [send(piece, perm=CORE_MOVE) for piece in cross]
    pool_other = send(pool, perm=BLK_MOVE)

    third = jnp.where(mp < 2, 2, 1)
    last = jnp.where(mp < 2, 3, 0)
    middle = (mp == 1) | (mp == 2)
    facts = [blk, middle, ring_half]
    for place_at in (mp, mp ^ 1, third, last):
        facts += [place_at, place_at // 2 != core, place_at % 2]
    facts += [prompt_len[0], page_count[0]]
    facts = jnp.stack([jnp.asarray(f, jnp.int32) for f in facts])
    facts = jnp.concatenate([facts, page_table[0]])
    so_far, last_w, server_q = query_part(
        facts, (tokens, near, mid_own, end_own), (*ring, *cross, *ring_other, *cross_other), token + late
    )
    own_q, send_q = zip(
        *(query_last(c * CUT, facts, mid_near[c], end_near[c], so_far, last_w) for c in range(2))
    )
    other_q = [send(piece, perm=BLK_MOVE) for piece in send_q]

    aligned = align(prompt_kv, kv_pool, pool_other)
    out = None
    for c in range(2):
        out = attend(
            c * CUT,
            kv_pool.shape[1],
            facts,
            own_q[c],
            other_q[c],
            aligned,
            out,
        )
    return (server_q, out)


def solution(mesh):
    in_specs = (
        P("dp", ("blk", "mp")),
        P(("mp", "blk"), "dp"),
        P(None, ("dp", "blk"), "mp"),
        P(None, ("dp", "blk"), "mp"),
        P(("dp", "blk"), None),
        P(("dp", "blk")),
        P(("dp", "blk")),
    )
    out_specs = (P("mp", "blk"), P(("dp", "blk"), "mp"))
    square = dict(mesh.shape) == {"dp": 4, "blk": 2, "mp": 4}
    return jax.shard_map(
        square_body if square else body,
        mesh=mesh,
        in_specs=in_specs,
        out_specs=out_specs,
        check_vma=False,
    )
```

```python
import functools

import jax
import jax.numpy as jnp
from jax import lax
from jax.experimental import pallas as pl
from jax.experimental.pallas import tpu as pltpu
from jax.sharding import PartitionSpec as P

HD = 224
PAGE = 16
W_PARTS = 1
CUT = 160
AXES = ("dp", "blk", "mp")
BF16 = jnp.bfloat16
F32 = jnp.float32
NT = (((1,), (1,)), ((), ()))


def attend_block(softmax_state, query_heads, key_heads, value_heads, key_mask):
    running_max, row_total, weighted = softmax_state
    scores = jnp.einsum(
        "thd,khd->htk", query_heads, key_heads, preferred_element_type=jnp.float32
    ) * HD ** (-0.5)
    scores = jnp.where(key_mask[None], scores, -1e30)
    new_max = jnp.maximum(running_max, jnp.max(scores, axis=2))
    weights = jnp.where(key_mask[None], jnp.exp(scores - new_max[:, :, None]), 0.0)
    factor = jnp.exp(running_max - new_max)
    row_total = row_total * factor + jnp.sum(weights, axis=2)
    weighted = weighted * factor[:, :, None] + jnp.einsum(
        "htk,khd->htd",
        weights.astype(jnp.bfloat16),
        value_heads,
        preferred_element_type=jnp.float32,
    )
    return (new_max, row_total, weighted)


def body(tokens, trainer_q, kv_pool, prompt_kv, page_table, page_count, prompt_len):
    trainer_rows = lax.all_gather(trainer_q.astype(jnp.bfloat16), "dp", axis=1, tiled=True)
    server_q = lax.all_to_all(trainer_rows, "blk", split_axis=1, concat_axis=0, tiled=True)
    features = lax.all_gather(tokens, "mp", axis=1, tiled=True)
    own_rows = features.shape[0] // lax.axis_size("blk")
    head_width = server_q.shape[0]
    token_local = lax.all_to_all(features, "blk", split_axis=0, concat_axis=1, tiled=True)
    queries = jnp.einsum(
        "td,hd->th",
        token_local,
        lax.all_gather(server_q, "blk", axis=1, tiled=True),
        preferred_element_type=jnp.float32,
    )
    queries = queries.astype(jnp.bfloat16)
    head_count = head_width // HD
    query_heads = queries.reshape(own_rows, head_count, HD)
    length = prompt_len[0]
    row_pages = page_table[0]
    live_slots = jnp.arange(row_pages.shape[0], dtype=jnp.int32) < page_count[0]
    row_index = jnp.arange(own_rows, dtype=jnp.int32)
    own_mask = (row_index[None, :] <= row_index[:, None]) & (row_index[None, :] < length)
    softmax_state = (
        jnp.full((head_count, own_rows), -1e30, jnp.float32),
        jnp.zeros((head_count, own_rows), jnp.float32),
        jnp.zeros((head_count, own_rows, HD), jnp.float32),
    )
    softmax_state = attend_block(
        softmax_state,
        query_heads,
        prompt_kv[0].reshape(own_rows, head_count, HD),
        prompt_kv[1].reshape(own_rows, head_count, HD),
        own_mask,
    )
    shard_piece = lax.all_gather(kv_pool, "blk", axis=1, tiled=True)
    key_count = shard_piece.shape[1]
    page_ids = jnp.arange(key_count, dtype=jnp.int32) // PAGE
    page_used = jnp.any((row_pages[None, :] == page_ids[:, None]) & live_slots[None, :], axis=1)
    key_mask = jnp.broadcast_to(page_used[None, :], (own_rows, key_count))
    running_max, row_total, weighted = attend_block(
        softmax_state,
        query_heads,
        shard_piece[0].reshape(key_count, head_count, HD),
        shard_piece[1].reshape(key_count, head_count, HD),
        key_mask,
    )
    mixed = weighted / row_total[:, :, None]
    mixed = jnp.where((row_index < length)[None, :, None], mixed, 0.0)
    mixed = jnp.transpose(mixed, (1, 0, 2)).reshape(own_rows, head_width).astype(jnp.bfloat16)
    return (server_q, mixed)


def pairs(move):
    def number(pair, core, blk, mp):
        return ((pair * 2 + core) * 2 + blk) * 4 + mp

    found = []
    for pair in range(2):
        for core in range(2):
            for blk in range(2):
                for mp in range(4):
                    target = move(pair, core, blk, mp)
                    if target is not None:
                        found.append((number(pair, core, blk, mp), number(*target)))
    return found


RING = {(0, 0): (1, 0), (1, 0): (1, 1), (1, 1): (0, 1), (0, 1): (0, 0)}
RING_MOVE = pairs(lambda p, c, b, m: (RING[p, b][0], c, RING[p, b][1], m))
CROSS_MOVE = pairs(lambda p, c, b, m: (p, c, b, m) if p == b else (b, c, p, m))
CORE_MOVE = pairs(lambda p, c, b, m: (p, 1 - c, b, m))
BLK_MOVE = pairs(lambda p, c, b, m: (p, c, 1 - b, m))
PAIR_MOVE = pairs(lambda p, c, b, m: (p, c, b, m ^ 1))
MID_MOVE = pairs(lambda p, c, b, m: (p, c, b, 3 - m) if m in (1, 2) else None)
END_MOVE = pairs(lambda p, c, b, m: (p, c, b, m ^ 1) if m in (1, 2) else None)


def cut_kernel(piece, *parts):
    half = piece.shape[0] // 2
    row = 0
    for part in parts:
        rows = part.shape[0] // 2
        for request in range(2):
            part[request * rows : (request + 1) * rows] = piece[
                request * half + row : request * half + row + rows
            ]
        row += rows


def cut(piece, first):
    rows, depth = piece.shape
    vmem = pl.BlockSpec(memory_space=pltpu.VMEM)
    return pl.pallas_call(
        cut_kernel,
        out_shape=(
            pltpu.VMEM((2 * first, depth), piece.dtype),
            pltpu.VMEM((rows - 2 * first, depth), piece.dtype),
        ),
        in_specs=[vmem],
        out_specs=(vmem, vmem),
        compiler_params=pltpu.CompilerParams(vmem_limit_bytes=8 * 1024 * 1024),
        cost_estimate=pl.CostEstimate(
            flops=0, bytes_accessed=4 * rows * depth, transcendentals=0
        ),
    )(piece)


def query_kernel(facts, *refs):
    wide = refs[:4]
    sides = (refs[4 : 4 + 2 * W_PARTS], refs[4 + 2 * W_PARTS : 4 + 4 * W_PARTS])
    total, last_w, server_q, held_t, held_w, got_t, got_w, put_w = refs[4 + 4 * W_PARTS + 1 :]
    middle, ring_half = facts[1], facts[2]
    rows, depth = sides[0][0].shape[0], held_w.shape[2]

    def fetch_t(k, source):
        return pltpu.make_async_copy(wide[k + source], held_t.at[k], got_t.at[k])

    def fetch_w(k, side, source):
        part = ring_half if source < W_PARTS else 1 - ring_half
        first_row = (part * W_PARTS + source % W_PARTS) * rows
        return pltpu.make_async_copy(
            sides[side][source].at[
                :, pl.ds(pl.multiple_of(facts[5 + 3 * k] * depth, 128), depth)
            ],
            held_w.at[k, pl.ds(pl.multiple_of(first_row, 16), rows)],
            got_w.at[k, source],
        )

    def store_w(k):
        return pltpu.make_async_copy(
            held_w.at[k],
            server_q.at[:, pl.ds(pl.multiple_of(facts[3 + 3 * k] * depth, 128), depth)],
            put_w.at[k],
        )

    for k in range(4):
        for side in range(2):

            @pl.when(facts[4 + 3 * k] == side)
            def _(k=k, side=side):
                for source in range(2 * W_PARTS):
                    fetch_w(k, side, source).start()

        if k < 2:
            fetch_t(k, 0).start()
        elif k == 2:
            for source in range(2):

                @pl.when(middle == 1 - source)
                def _(k=k, source=source):
                    fetch_t(k, source).start()

    for k in range(4):
        for source in range(2 * W_PARTS):
            fetch_w(k, 0, source).wait()
        store_w(k).start()
        if k == 3:
            last_w[...] = held_w[k]
        else:
            fetch_t(k, 0).wait()
            part = lax.dot_general(held_t[k], held_w[k], NT, preferred_element_type=F32)
            if k == 0:
                total[...] = part
            else:
                total[...] += part
    for k in range(4):
        store_w(k).wait()


def query_part(facts, wide, sides, token):
    rows, depth = wide[0].shape
    heads = 2 * W_PARTS * sides[0].shape[0]
    in_hbm = functools.partial(pltpu.with_memory_space_constraint, memory_space=pltpu.HBM)
    wide = [in_hbm(piece) for piece in wide]
    sides = [in_hbm(piece) for piece in sides]
    vmem = pl.BlockSpec(memory_space=pltpu.VMEM)
    anywhere = pl.BlockSpec(memory_space=pl.ANY)
    return pl.pallas_call(
        query_kernel,
        out_shape=(
            pltpu.VMEM((rows, heads), F32),
            pltpu.VMEM((heads, depth), BF16),
            jax.ShapeDtypeStruct((heads, 4 * depth), BF16),
        ),
        in_specs=[pl.BlockSpec(memory_space=pltpu.SMEM)] + [anywhere] * (4 + 4 * W_PARTS + 1),
        out_specs=(vmem, vmem, anywhere),
        scratch_shapes=[
            pltpu.VMEM((3, rows, depth), BF16),
            pltpu.VMEM((4, heads, depth), BF16),
            pltpu.SemaphoreType.DMA((3,)),
            pltpu.SemaphoreType.DMA((4, 2 * W_PARTS)),
            pltpu.SemaphoreType.DMA((4,)),
        ],
        compiler_params=pltpu.CompilerParams(vmem_limit_bytes=14 * 1024 * 1024),
        cost_estimate=pl.CostEstimate(
            flops=2 * 3 * rows * depth * heads,
            bytes_accessed=2 * 4 * (rows + 2 * heads) * depth,
            transcendentals=0,
        ),
    )(facts, *wide, *sides, *token)


def last_kernel(first_row, facts, mid_piece, end_piece, so_far, weights, own, send):
    middle, blk = facts[1], facts[0]
    half = own.shape[0]
    piece = jnp.where(middle == 1, mid_piece[...], end_piece[...])
    part = lax.dot_general(piece, weights[...], NT, preferred_element_type=F32)
    whole = so_far.shape[0] // 2
    upper = so_far[first_row : first_row + half] + part[:half]
    lower = so_far[whole + first_row : whole + first_row + half] + part[half:]

    @pl.when(blk == 0)
    def _():
        own[...] = upper
        send[...] = lower.astype(BF16)

    @pl.when(blk == 1)
    def _():
        own[...] = lower
        send[...] = upper.astype(BF16)


def query_last(first_row, facts, mid_piece, end_piece, so_far, weights):
    rows, depth = mid_piece.shape
    heads = weights.shape[0]
    vmem = pl.BlockSpec(memory_space=pltpu.VMEM)
    return pl.pallas_call(
        functools.partial(last_kernel, first_row),
        out_shape=(
            jax.ShapeDtypeStruct((rows // 2, heads), F32),
            jax.ShapeDtypeStruct((rows // 2, heads), BF16),
        ),
        in_specs=[pl.BlockSpec(memory_space=pltpu.SMEM)] + [vmem] * 4,
        out_specs=(vmem,) * 2,
        compiler_params=pltpu.CompilerParams(vmem_limit_bytes=6 * 1024 * 1024),
        cost_estimate=pl.CostEstimate(
            flops=2 * rows * depth * heads,
            bytes_accessed=2 * (2 * rows + heads) * depth,
            transcendentals=0,
        ),
    )(facts, mid_piece, end_piece, so_far, weights)


def window(head, width):
    low = head * HD // 128 * 128
    high = min(width, -(-(head + 1) * HD // 128) * 128)
    return low, high, head * HD - low


def to_front(wide, offset):
    if offset:
        wide = pltpu.roll(wide, wide.shape[1] - offset, 1)
    return wide[:, :256]


def align_kernel(prompt, pool_own, pool_other, out):
    width = prompt.shape[2]
    for kind in range(2):
        row = 0
        for ref in (pool_own, pool_other, prompt):
            rows = ref.shape[1]
            for head in range(width // HD):
                low, high, offset = window(head, width)
                wide = ref[kind, :, low:high].astype(F32)
                out[kind, head, row : row + rows] = to_front(wide, offset).astype(BF16)
            row += rows


def align(prompt, pool_own, pool_other):
    width = prompt.shape[2]
    keys = prompt.shape[1] + pool_own.shape[1] + pool_other.shape[1]
    vmem = pl.BlockSpec(memory_space=pltpu.VMEM)
    return pl.pallas_call(
        align_kernel,
        out_shape=jax.ShapeDtypeStruct((2, width // HD, keys, 256), BF16),
        in_specs=[vmem] * 3,
        out_specs=vmem,
        compiler_params=pltpu.CompilerParams(vmem_limit_bytes=12 * 1024 * 1024),
        cost_estimate=pl.CostEstimate(
            flops=0, bytes_accessed=8 * keys * width, transcendentals=0
        ),
    )(prompt, pool_own, pool_other)


def attend_kernel(first_row, pool_keys, facts, own_q, other_q, aligned, *refs):
    out, done, sem = refs[-3:]
    rows, width = done.shape
    heads = width // HD
    length, page_total, blk = facts[15], facts[16], facts[0]
    query = (own_q[...] + other_q[...].astype(F32)).astype(BF16).astype(F32)

    keys = 2 * pool_keys + first_row + rows
    key_at = lax.broadcasted_iota(jnp.int32, (1, keys), 1)
    own_side = key_at < pool_keys
    pages_here = pool_keys // PAGE
    page = jnp.where(own_side, blk, -blk) * pages_here + key_at // PAGE
    used = jnp.zeros((1, keys), jnp.int32)
    for slot in range(facts.shape[0] - 17):
        used = jnp.where((page == facts[17 + slot]) & (slot < page_total), 1, used)
    prompt_at = key_at - 2 * pool_keys
    seen_from = jnp.where(
        prompt_at >= 0,
        jnp.where(prompt_at < length, prompt_at, first_row + rows),
        jnp.where(used > 0, 0, first_row + rows),
    )
    row_at = first_row + lax.broadcasted_iota(jnp.int32, (rows, 1), 0)
    seen = seen_from <= row_at
    live = row_at < length
    lanes = lax.broadcasted_iota(jnp.int32, (1, 256), 1)

    raw = []
    for head in range(heads):
        low, high, offset = window(head, width)
        head_q = jnp.where(lanes < HD, to_front(query[:, low:high], offset), 0.0).astype(BF16)
        raw.append(
            lax.dot_general(head_q, aligned[0, head, :keys], NT, preferred_element_type=F32)
        )
    tiles = [None] * (width // 128)
    for head in range(heads):
        low, high, offset = window(head, width)
        scores = jnp.where(seen, raw[head] * HD**-0.5, -1e30)
        weights = jnp.exp(scores - jnp.max(scores, axis=1, keepdims=True))
        total = jnp.sum(weights, axis=1, keepdims=True)
        value = jnp.dot(
            weights.astype(BF16), aligned[1, head, :keys], preferred_element_type=F32
        )
        value = jnp.where(live, value * (1.0 / total), 0.0)
        if high - low > 256:
            value = jnp.concatenate([value, jnp.zeros((rows, high - low - 256), F32)], axis=1)
        if offset:
            value = pltpu.roll(value, offset, 1)
        for tile in range(low // 128, high // 128):
            part = value[:, tile * 128 - low : (tile + 1) * 128 - low]
            if tiles[tile] is None:
                tiles[tile] = part
            else:
                tiles[tile] = jnp.where(
                    lanes[:, :128] < head * HD - tile * 128, tiles[tile], part
                )
    for tile, part in enumerate(tiles):
        done[:, tile * 128 : (tile + 1) * 128] = part.astype(BF16)
    copy = pltpu.make_async_copy(done, out.at[pl.ds(first_row, rows)], sem)
    copy.start()
    copy.wait()


def attend(first_row, pool_keys, facts, own_q, other_q, aligned, before=None):
    rows, width = own_q.shape
    all_rows = aligned.shape[2] - 2 * pool_keys
    smem = pl.BlockSpec(memory_space=pltpu.SMEM)
    vmem = pl.BlockSpec(memory_space=pltpu.VMEM)
    in_specs = [smem] + [vmem] * 3
    operands = [facts, own_q, other_q, aligned]
    if before is not None:
        in_specs.append(pl.BlockSpec(memory_space=pl.ANY))
        operands.append(before)
    return pl.pallas_call(
        functools.partial(attend_kernel, first_row, pool_keys),
        out_shape=jax.ShapeDtypeStruct((all_rows, width), BF16),
        in_specs=in_specs,
        out_specs=pl.BlockSpec(memory_space=pl.ANY),
        scratch_shapes=[
            pltpu.VMEM((rows, width), BF16),
            pltpu.SemaphoreType.DMA(()),
        ],
        input_output_aliases={} if before is None else {4: 0},
        compiler_params=pltpu.CompilerParams(vmem_limit_bytes=8 * 1024 * 1024),
        cost_estimate=pl.CostEstimate(
            flops=4 * rows * 512 * width, bytes_accessed=8 * 512 * width, transcendentals=rows * 2048
        ),
    )(*operands)


def square_body(tokens, trainer_q, kv_pool, prompt_kv, page_table, page_count, prompt_len):
    dp, blk, mp = (lax.axis_index(name) for name in AXES)
    core, ring_half = dp % 2, 1 - dp // 2
    send = functools.partial(lax.ppermute, axis_name=AXES)

    near = send(tokens, perm=PAIR_MOVE)
    mid_own = send(tokens, perm=MID_MOVE)
    end_own = send(mid_own, perm=END_MOVE)
    parts = cut(near, CUT)
    mid_near = [send(parts[0], perm=MID_MOVE)]
    mid_near.append(send(parts[1], perm=MID_MOVE))
    end_near = [send(piece, perm=END_MOVE) for piece in mid_near]

    token = []
    late = []
    piece = mid_near[0][:192]
    for _ in range(1):
        piece = send(piece, perm=CORE_MOVE)
    token.append(piece)
    rows = trainer_q.shape[0] // W_PARTS
    own_w = [trainer_q[p * rows : (p + 1) * rows].astype(BF16) for p in range(W_PARTS)]
    ring = [send(piece, perm=RING_MOVE) for piece in own_w]
    cross = [send(piece, perm=CROSS_MOVE) for piece in own_w]
    ring, cross, token, _ = lax.optimization_barrier((ring, cross, token, (end_own, mid_near[0], mid_near[1], )))
    pool = kv_pool
    pool, _ = lax.optimization_barrier((kv_pool, (ring,)))
    ring_other = [send(piece, perm=CORE_MOVE) for piece in ring]
    cross_other = [send(piece, perm=CORE_MOVE) for piece in cross]
    pool_other = send(pool, perm=BLK_MOVE)

    third = jnp.where(mp < 2, 2, 1)
    last = jnp.where(mp < 2, 3, 0)
    middle = (mp == 1) | (mp == 2)
    facts = [blk, middle, ring_half]
    for place_at in (mp, mp ^ 1, third, last):
        facts += [place_at, place_at // 2 != core, place_at % 2]
    facts += [prompt_len[0], page_count[0]]
    facts = jnp.stack([jnp.asarray(f, jnp.int32) for f in facts])
    facts = jnp.concatenate([facts, page_table[0]])
    so_far, last_w, server_q = query_part(
        facts, (tokens, near, mid_own, end_own), (*ring, *cross, *ring_other, *cross_other), token + late
    )
    own_q, send_q = zip(
        *(query_last(c * CUT, facts, mid_near[c], end_near[c], so_far, last_w) for c in range(2))
    )
    other_q = [send(piece, perm=BLK_MOVE) for piece in send_q]

    aligned = align(prompt_kv, kv_pool, pool_other)
    out = None
    for c in range(2):
        out = attend(
            c * CUT,
            kv_pool.shape[1],
            facts,
            own_q[c],
            other_q[c],
            aligned,
            out,
        )
    return (server_q, out)


def solution(mesh):
    in_specs = (
        P("dp", ("blk", "mp")),
        P(("mp", "blk"), "dp"),
        P(None, ("dp", "blk"), "mp"),
        P(None, ("dp", "blk"), "mp"),
        P(("dp", "blk"), None),
        P(("dp", "blk")),
        P(("dp", "blk")),
    )
    out_specs = (P("mp", "blk"), P(("dp", "blk"), "mp"))
    square = dict(mesh.shape) == {"dp": 4, "blk": 2, "mp": 4}
    return jax.shard_map(
        square_body if square else body,
        mesh=mesh,
        in_specs=in_specs,
        out_specs=out_specs,
        check_vma=False,
    )
```

```python
import functools

import jax
import jax.numpy as jnp
from jax import lax
from jax.experimental import pallas as pl
from jax.experimental.pallas import tpu as pltpu
from jax.sharding import PartitionSpec as P

HD = 224
PAGE = 16
W_PARTS = 1
CUT = 160
AXES = ("dp", "blk", "mp")
BF16 = jnp.bfloat16
F32 = jnp.float32
NT = (((1,), (1,)), ((), ()))


def attend_block(softmax_state, query_heads, key_heads, value_heads, key_mask):
    running_max, row_total, weighted = softmax_state
    scores = jnp.einsum(
        "thd,khd->htk", query_heads, key_heads, preferred_element_type=jnp.float32
    ) * HD ** (-0.5)
    scores = jnp.where(key_mask[None], scores, -1e30)
    new_max = jnp.maximum(running_max, jnp.max(scores, axis=2))
    weights = jnp.where(key_mask[None], jnp.exp(scores - new_max[:, :, None]), 0.0)
    factor = jnp.exp(running_max - new_max)
    row_total = row_total * factor + jnp.sum(weights, axis=2)
    weighted = weighted * factor[:, :, None] + jnp.einsum(
        "htk,khd->htd",
        weights.astype(jnp.bfloat16),
        value_heads,
        preferred_element_type=jnp.float32,
    )
    return (new_max, row_total, weighted)


def body(tokens, trainer_q, kv_pool, prompt_kv, page_table, page_count, prompt_len):
    trainer_rows = lax.all_gather(trainer_q.astype(jnp.bfloat16), "dp", axis=1, tiled=True)
    server_q = lax.all_to_all(trainer_rows, "blk", split_axis=1, concat_axis=0, tiled=True)
    features = lax.all_gather(tokens, "mp", axis=1, tiled=True)
    own_rows = features.shape[0] // lax.axis_size("blk")
    head_width = server_q.shape[0]
    token_local = lax.all_to_all(features, "blk", split_axis=0, concat_axis=1, tiled=True)
    queries = jnp.einsum(
        "td,hd->th",
        token_local,
        lax.all_gather(server_q, "blk", axis=1, tiled=True),
        preferred_element_type=jnp.float32,
    )
    queries = queries.astype(jnp.bfloat16)
    head_count = head_width // HD
    query_heads = queries.reshape(own_rows, head_count, HD)
    length = prompt_len[0]
    row_pages = page_table[0]
    live_slots = jnp.arange(row_pages.shape[0], dtype=jnp.int32) < page_count[0]
    row_index = jnp.arange(own_rows, dtype=jnp.int32)
    own_mask = (row_index[None, :] <= row_index[:, None]) & (row_index[None, :] < length)
    softmax_state = (
        jnp.full((head_count, own_rows), -1e30, jnp.float32),
        jnp.zeros((head_count, own_rows), jnp.float32),
        jnp.zeros((head_count, own_rows, HD), jnp.float32),
    )
    softmax_state = attend_block(
        softmax_state,
        query_heads,
        prompt_kv[0].reshape(own_rows, head_count, HD),
        prompt_kv[1].reshape(own_rows, head_count, HD),
        own_mask,
    )
    shard_piece = lax.all_gather(kv_pool, "blk", axis=1, tiled=True)
    key_count = shard_piece.shape[1]
    page_ids = jnp.arange(key_count, dtype=jnp.int32) // PAGE
    page_used = jnp.any((row_pages[None, :] == page_ids[:, None]) & live_slots[None, :], axis=1)
    key_mask = jnp.broadcast_to(page_used[None, :], (own_rows, key_count))
    running_max, row_total, weighted = attend_block(
        softmax_state,
        query_heads,
        shard_piece[0].reshape(key_count, head_count, HD),
        shard_piece[1].reshape(key_count, head_count, HD),
        key_mask,
    )
    mixed = weighted / row_total[:, :, None]
    mixed = jnp.where((row_index < length)[None, :, None], mixed, 0.0)
    mixed = jnp.transpose(mixed, (1, 0, 2)).reshape(own_rows, head_width).astype(jnp.bfloat16)
    return (server_q, mixed)


def pairs(move):
    def number(pair, core, blk, mp):
        return ((pair * 2 + core) * 2 + blk) * 4 + mp

    found = []
    for pair in range(2):
        for core in range(2):
            for blk in range(2):
                for mp in range(4):
                    target = move(pair, core, blk, mp)
                    if target is not None:
                        found.append((number(pair, core, blk, mp), number(*target)))
    return found


RING = {(0, 0): (1, 0), (1, 0): (1, 1), (1, 1): (0, 1), (0, 1): (0, 0)}
RING_MOVE = pairs(lambda p, c, b, m: (RING[p, b][0], c, RING[p, b][1], m))
CROSS_MOVE = pairs(lambda p, c, b, m: (p, c, b, m) if p == b else (b, c, p, m))
CORE_MOVE = pairs(lambda p, c, b, m: (p, 1 - c, b, m))
BLK_MOVE = pairs(lambda p, c, b, m: (p, c, 1 - b, m))
PAIR_MOVE = pairs(lambda p, c, b, m: (p, c, b, m ^ 1))
MID_MOVE = pairs(lambda p, c, b, m: (p, c, b, 3 - m) if m in (1, 2) else None)
END_MOVE = pairs(lambda p, c, b, m: (p, c, b, m ^ 1) if m in (1, 2) else None)


def cut_kernel(piece, *parts):
    half = piece.shape[0] // 2
    row = 0
    for part in parts:
        rows = part.shape[0] // 2
        for request in range(2):
            part[request * rows : (request + 1) * rows] = piece[
                request * half + row : request * half + row + rows
            ]
        row += rows


def cut(piece, first):
    rows, depth = piece.shape
    vmem = pl.BlockSpec(memory_space=pltpu.VMEM)
    return pl.pallas_call(
        cut_kernel,
        out_shape=(
            pltpu.VMEM((2 * first, depth), piece.dtype),
            pltpu.VMEM((rows - 2 * first, depth), piece.dtype),
        ),
        in_specs=[vmem],
        out_specs=(vmem, vmem),
        compiler_params=pltpu.CompilerParams(vmem_limit_bytes=8 * 1024 * 1024),
        cost_estimate=pl.CostEstimate(
            flops=0, bytes_accessed=4 * rows * depth, transcendentals=0
        ),
    )(piece)


def query_kernel(facts, *refs):
    wide = refs[:4]
    sides = (refs[4 : 4 + 2 * W_PARTS], refs[4 + 2 * W_PARTS : 4 + 4 * W_PARTS])
    total, last_w, server_q, held_t, held_w, got_t, got_w, put_w = refs[4 + 4 * W_PARTS + 1 :]
    middle, ring_half = facts[1], facts[2]
    rows, depth = sides[0][0].shape[0], held_w.shape[2]

    def fetch_t(k, source):
        return pltpu.make_async_copy(wide[k + source], held_t.at[k], got_t.at[k])

    def fetch_w(k, side, source):
        part = ring_half if source < W_PARTS else 1 - ring_half
        first_row = (part * W_PARTS + source % W_PARTS) * rows
        return pltpu.make_async_copy(
            sides[side][source].at[
                :, pl.ds(pl.multiple_of(facts[5 + 3 * k] * depth, 128), depth)
            ],
            held_w.at[k, pl.ds(pl.multiple_of(first_row, 16), rows)],
            got_w.at[k, source],
        )

    def store_w(k):
        return pltpu.make_async_copy(
            held_w.at[k],
            server_q.at[:, pl.ds(pl.multiple_of(facts[3 + 3 * k] * depth, 128), depth)],
            put_w.at[k],
        )

    for k in range(4):
        for side in range(2):

            @pl.when(facts[4 + 3 * k] == side)
            def _(k=k, side=side):
                for source in range(2 * W_PARTS):
                    fetch_w(k, side, source).start()

        if k < 2:
            fetch_t(k, 0).start()
        elif k == 2:
            for source in range(2):

                @pl.when(middle == 1 - source)
                def _(k=k, source=source):
                    fetch_t(k, source).start()

    for k in range(4):
        for source in range(2 * W_PARTS):
            fetch_w(k, 0, source).wait()
        store_w(k).start()
        if k == 3:
            last_w[...] = held_w[k]
        else:
            fetch_t(k, 0).wait()
            part = lax.dot_general(held_t[k], held_w[k], NT, preferred_element_type=F32)
            if k == 0:
                total[...] = part
            else:
                total[...] += part
    for k in range(4):
        store_w(k).wait()


def query_part(facts, wide, sides, token):
    rows, depth = wide[0].shape
    heads = 2 * W_PARTS * sides[0].shape[0]
    in_hbm = functools.partial(pltpu.with_memory_space_constraint, memory_space=pltpu.HBM)
    wide = [in_hbm(piece) for piece in wide]
    sides = [in_hbm(piece) for piece in sides]
    vmem = pl.BlockSpec(memory_space=pltpu.VMEM)
    anywhere = pl.BlockSpec(memory_space=pl.ANY)
    return pl.pallas_call(
        query_kernel,
        out_shape=(
            pltpu.VMEM((rows, heads), F32),
            pltpu.VMEM((heads, depth), BF16),
            jax.ShapeDtypeStruct((heads, 4 * depth), BF16),
        ),
        in_specs=[pl.BlockSpec(memory_space=pltpu.SMEM)] + [anywhere] * (4 + 4 * W_PARTS + 1),
        out_specs=(vmem, vmem, anywhere),
        scratch_shapes=[
            pltpu.VMEM((3, rows, depth), BF16),
            pltpu.VMEM((4, heads, depth), BF16),
            pltpu.SemaphoreType.DMA((3,)),
            pltpu.SemaphoreType.DMA((4, 2 * W_PARTS)),
            pltpu.SemaphoreType.DMA((4,)),
        ],
        compiler_params=pltpu.CompilerParams(vmem_limit_bytes=14 * 1024 * 1024),
        cost_estimate=pl.CostEstimate(
            flops=2 * 3 * rows * depth * heads,
            bytes_accessed=2 * 4 * (rows + 2 * heads) * depth,
            transcendentals=0,
        ),
    )(facts, *wide, *sides, *token)


def last_kernel(first_row, facts, mid_piece, end_piece, so_far, weights, own, send):
    middle, blk = facts[1], facts[0]
    half = own.shape[0]
    piece = jnp.where(middle == 1, mid_piece[...], end_piece[...])
    part = lax.dot_general(piece, weights[...], NT, preferred_element_type=F32)
    whole = so_far.shape[0] // 2
    upper = so_far[first_row : first_row + half] + part[:half]
    lower = so_far[whole + first_row : whole + first_row + half] + part[half:]

    @pl.when(blk == 0)
    def _():
        own[...] = upper
        send[...] = lower.astype(BF16)

    @pl.when(blk == 1)
    def _():
        own[...] = lower
        send[...] = upper.astype(BF16)


def side_kernel(first_row, sent, facts, mid_piece, end_piece, so_far, weights, out):
    half, whole = out.shape[0], so_far.shape[0] // 2
    request = 1 - facts[0] if sent else facts[0]
    here = pl.ds(pl.multiple_of(request * half, 16), half)
    piece = jnp.where(facts[1] == 1, mid_piece[here, :], end_piece[here, :])
    part = lax.dot_general(piece, weights[...], NT, preferred_element_type=F32)
    before = so_far[pl.ds(pl.multiple_of(request * whole + first_row, 16), half), :]
    out[...] = (before + part).astype(out.dtype)


def query_side(first_row, sent, facts, mid_piece, end_piece, so_far, weights):
    rows, depth = mid_piece.shape
    heads = weights.shape[0]
    vmem = pl.BlockSpec(memory_space=pltpu.VMEM)
    return pl.pallas_call(
        functools.partial(side_kernel, first_row, sent),
        out_shape=jax.ShapeDtypeStruct((rows // 2, heads), BF16 if sent else F32),
        in_specs=[pl.BlockSpec(memory_space=pltpu.SMEM)] + [vmem] * 4,
        out_specs=vmem,
        compiler_params=pltpu.CompilerParams(vmem_limit_bytes=6 * 1024 * 1024),
        cost_estimate=pl.CostEstimate(
            flops=rows * depth * heads,
            bytes_accessed=2 * (rows + heads) * depth,
            transcendentals=0,
        ),
    )(facts, mid_piece, end_piece, so_far, weights)


def query_last(first_row, facts, mid_piece, end_piece, so_far, weights):
    rows, depth = mid_piece.shape
    heads = weights.shape[0]
    vmem = pl.BlockSpec(memory_space=pltpu.VMEM)
    return pl.pallas_call(
        functools.partial(last_kernel, first_row),
        out_shape=(
            jax.ShapeDtypeStruct((rows // 2, heads), F32),
            jax.ShapeDtypeStruct((rows // 2, heads), BF16),
        ),
        in_specs=[pl.BlockSpec(memory_space=pltpu.SMEM)] + [vmem] * 4,
        out_specs=(vmem,) * 2,
        compiler_params=pltpu.CompilerParams(vmem_limit_bytes=6 * 1024 * 1024),
        cost_estimate=pl.CostEstimate(
            flops=2 * rows * depth * heads,
            bytes_accessed=2 * (2 * rows + heads) * depth,
            transcendentals=0,
        ),
    )(facts, mid_piece, end_piece, so_far, weights)


def window(head, width):
    low = head * HD // 128 * 128
    high = min(width, -(-(head + 1) * HD // 128) * 128)
    return low, high, head * HD - low


def to_front(wide, offset):
    if offset:
        wide = pltpu.roll(wide, wide.shape[1] - offset, 1)
    return wide[:, :256]


def align_kernel(prompt, pool_own, pool_other, out):
    width = prompt.shape[2]
    for kind in range(2):
        row = 0
        for ref in (pool_own, pool_other, prompt):
            rows = ref.shape[1]
            for head in range(width // HD):
                low, high, offset = window(head, width)
                wide = ref[kind, :, low:high].astype(F32)
                out[kind, head, row : row + rows] = to_front(wide, offset).astype(BF16)
            row += rows


def align(prompt, pool_own, pool_other):
    width = prompt.shape[2]
    keys = prompt.shape[1] + pool_own.shape[1] + pool_other.shape[1]
    vmem = pl.BlockSpec(memory_space=pltpu.VMEM)
    return pl.pallas_call(
        align_kernel,
        out_shape=jax.ShapeDtypeStruct((2, width // HD, keys, 256), BF16),
        in_specs=[vmem] * 3,
        out_specs=vmem,
        compiler_params=pltpu.CompilerParams(vmem_limit_bytes=12 * 1024 * 1024),
        cost_estimate=pl.CostEstimate(
            flops=0, bytes_accessed=8 * keys * width, transcendentals=0
        ),
    )(prompt, pool_own, pool_other)


def attend_kernel(first_row, pool_keys, facts, own_q, other_q, aligned, *refs):
    out, done, sem = refs[-3:]
    rows, width = done.shape
    heads = width // HD
    length, page_total, blk = facts[15], facts[16], facts[0]
    query = (own_q[...] + other_q[...].astype(F32)).astype(BF16).astype(F32)

    keys = 2 * pool_keys + first_row + rows
    key_at = lax.broadcasted_iota(jnp.int32, (1, keys), 1)
    own_side = key_at < pool_keys
    pages_here = pool_keys // PAGE
    page = jnp.where(own_side, blk, -blk) * pages_here + key_at // PAGE
    used = jnp.zeros((1, keys), jnp.int32)
    for slot in range(facts.shape[0] - 17):
        used = jnp.where((page == facts[17 + slot]) & (slot < page_total), 1, used)
    prompt_at = key_at - 2 * pool_keys
    seen_from = jnp.where(
        prompt_at >= 0,
        jnp.where(prompt_at < length, prompt_at, first_row + rows),
        jnp.where(used > 0, 0, first_row + rows),
    )
    row_at = first_row + lax.broadcasted_iota(jnp.int32, (rows, 1), 0)
    seen = seen_from <= row_at
    live = row_at < length
    lanes = lax.broadcasted_iota(jnp.int32, (1, 256), 1)

    raw = []
    for head in range(heads):
        low, high, offset = window(head, width)
        head_q = jnp.where(lanes < HD, to_front(query[:, low:high], offset), 0.0).astype(BF16)
        raw.append(
            lax.dot_general(head_q, aligned[0, head, :keys], NT, preferred_element_type=F32)
        )
    tiles = [None] * (width // 128)
    for head in range(heads):
        low, high, offset = window(head, width)
        scores = jnp.where(seen, raw[head] * HD**-0.5, -1e30)
        weights = jnp.exp(scores - jnp.max(scores, axis=1, keepdims=True))
        total = jnp.sum(weights, axis=1, keepdims=True)
        value = jnp.dot(
            weights.astype(BF16), aligned[1, head, :keys], preferred_element_type=F32
        )
        value = jnp.where(live, value * (1.0 / total), 0.0)
        if high - low > 256:
            value = jnp.concatenate([value, jnp.zeros((rows, high - low - 256), F32)], axis=1)
        if offset:
            value = pltpu.roll(value, offset, 1)
        for tile in range(low // 128, high // 128):
            part = value[:, tile * 128 - low : (tile + 1) * 128 - low]
            if tiles[tile] is None:
                tiles[tile] = part
            else:
                tiles[tile] = jnp.where(
                    lanes[:, :128] < head * HD - tile * 128, tiles[tile], part
                )
    for tile, part in enumerate(tiles):
        done[:, tile * 128 : (tile + 1) * 128] = part.astype(BF16)
    copy = pltpu.make_async_copy(done, out.at[pl.ds(first_row, rows)], sem)
    copy.start()
    copy.wait()


def attend(first_row, pool_keys, facts, own_q, other_q, aligned, before=None):
    rows, width = own_q.shape
    all_rows = aligned.shape[2] - 2 * pool_keys
    smem = pl.BlockSpec(memory_space=pltpu.SMEM)
    vmem = pl.BlockSpec(memory_space=pltpu.VMEM)
    in_specs = [smem] + [vmem] * 3
    operands = [facts, own_q, other_q, aligned]
    if before is not None:
        in_specs.append(pl.BlockSpec(memory_space=pl.ANY))
        operands.append(before)
    return pl.pallas_call(
        functools.partial(attend_kernel, first_row, pool_keys),
        out_shape=jax.ShapeDtypeStruct((all_rows, width), BF16),
        in_specs=in_specs,
        out_specs=pl.BlockSpec(memory_space=pl.ANY),
        scratch_shapes=[
            pltpu.VMEM((rows, width), BF16),
            pltpu.SemaphoreType.DMA(()),
        ],
        input_output_aliases={} if before is None else {4: 0},
        compiler_params=pltpu.CompilerParams(vmem_limit_bytes=8 * 1024 * 1024),
        cost_estimate=pl.CostEstimate(
            flops=4 * rows * 512 * width, bytes_accessed=8 * 512 * width, transcendentals=rows * 2048
        ),
    )(*operands)


def square_body(tokens, trainer_q, kv_pool, prompt_kv, page_table, page_count, prompt_len):
    dp, blk, mp = (lax.axis_index(name) for name in AXES)
    core, ring_half = dp % 2, 1 - dp // 2
    send = functools.partial(lax.ppermute, axis_name=AXES)

    near = send(tokens, perm=PAIR_MOVE)
    mid_own = send(tokens, perm=MID_MOVE)
    end_own = send(mid_own, perm=END_MOVE)
    parts = cut(near, CUT)
    mid_near = [send(parts[0], perm=MID_MOVE)]
    mid_near.append(send(parts[1], perm=MID_MOVE))
    end_near = [send(piece, perm=END_MOVE) for piece in mid_near]

    token = []
    late = []
    piece = mid_near[0][:192]
    for _ in range(1):
        piece = send(piece, perm=CORE_MOVE)
    token.append(piece)
    rows = trainer_q.shape[0] // W_PARTS
    own_w = [trainer_q[p * rows : (p + 1) * rows].astype(BF16) for p in range(W_PARTS)]
    ring = [send(piece, perm=RING_MOVE) for piece in own_w]
    cross = [send(piece, perm=CROSS_MOVE) for piece in own_w]
    ring, cross, token, _ = lax.optimization_barrier((ring, cross, token, (end_own, mid_near[0], mid_near[1], )))
    pool = kv_pool
    pool, _ = lax.optimization_barrier((kv_pool, (ring,)))
    ring_other = [send(piece, perm=CORE_MOVE) for piece in ring]
    cross_other = [send(piece, perm=CORE_MOVE) for piece in cross]
    pool_other = send(pool, perm=BLK_MOVE)

    third = jnp.where(mp < 2, 2, 1)
    last = jnp.where(mp < 2, 3, 0)
    middle = (mp == 1) | (mp == 2)
    facts = [blk, middle, ring_half]
    for place_at in (mp, mp ^ 1, third, last):
        facts += [place_at, place_at // 2 != core, place_at % 2]
    facts += [prompt_len[0], page_count[0]]
    facts = jnp.stack([jnp.asarray(f, jnp.int32) for f in facts])
    facts = jnp.concatenate([facts, page_table[0]])
    so_far, last_w, server_q = query_part(
        facts, (tokens, near, mid_own, end_own), (*ring, *cross, *ring_other, *cross_other), token + late
    )
    first_own, first_send = query_last(0, facts, mid_near[0], end_near[0], so_far, last_w)
    last_own, last_send = (
        query_side(CUT, sent, facts, mid_near[1], end_near[1], so_far, last_w)
        for sent in (False, True)
    )
    own_q, send_q = (first_own, last_own), (first_send, last_send)
    other_q = [send(piece, perm=BLK_MOVE) for piece in send_q]

    aligned = align(prompt_kv, kv_pool, pool_other)
    out = None
    for c in range(2):
        out = attend(
            c * CUT,
            kv_pool.shape[1],
            facts,
            own_q[c],
            other_q[c],
            aligned,
            out,
        )
    return (server_q, out)


def solution(mesh):
    in_specs = (
        P("dp", ("blk", "mp")),
        P(("mp", "blk"), "dp"),
        P(None, ("dp", "blk"), "mp"),
        P(None, ("dp", "blk"), "mp"),
        P(("dp", "blk"), None),
        P(("dp", "blk")),
        P(("dp", "blk")),
    )
    out_specs = (P("mp", "blk"), P(("dp", "blk"), "mp"))
    square = dict(mesh.shape) == {"dp": 4, "blk": 2, "mp": 4}
    return jax.shard_map(
        square_body if square else body,
        mesh=mesh,
        in_specs=in_specs,
        out_specs=out_specs,
        check_vma=False,
    )
```

```python
import functools

import jax
import jax.numpy as jnp
from jax import lax
from jax.experimental import pallas as pl
from jax.experimental.pallas import tpu as pltpu
from jax.sharding import PartitionSpec as P

HD = 224
PAGE = 16
W_PARTS = 1
CUT = 160
AXES = ("dp", "blk", "mp")
BF16 = jnp.bfloat16
F32 = jnp.float32
NT = (((1,), (1,)), ((), ()))


def attend_block(softmax_state, query_heads, key_heads, value_heads, key_mask):
    running_max, row_total, weighted = softmax_state
    scores = jnp.einsum(
        "thd,khd->htk", query_heads, key_heads, preferred_element_type=jnp.float32
    ) * HD ** (-0.5)
    scores = jnp.where(key_mask[None], scores, -1e30)
    new_max = jnp.maximum(running_max, jnp.max(scores, axis=2))
    weights = jnp.where(key_mask[None], jnp.exp(scores - new_max[:, :, None]), 0.0)
    factor = jnp.exp(running_max - new_max)
    row_total = row_total * factor + jnp.sum(weights, axis=2)
    weighted = weighted * factor[:, :, None] + jnp.einsum(
        "htk,khd->htd",
        weights.astype(jnp.bfloat16),
        value_heads,
        preferred_element_type=jnp.float32,
    )
    return (new_max, row_total, weighted)


def body(tokens, trainer_q, kv_pool, prompt_kv, page_table, page_count, prompt_len):
    trainer_rows = lax.all_gather(trainer_q.astype(jnp.bfloat16), "dp", axis=1, tiled=True)
    server_q = lax.all_to_all(trainer_rows, "blk", split_axis=1, concat_axis=0, tiled=True)
    features = lax.all_gather(tokens, "mp", axis=1, tiled=True)
    own_rows = features.shape[0] // lax.axis_size("blk")
    head_width = server_q.shape[0]
    token_local = lax.all_to_all(features, "blk", split_axis=0, concat_axis=1, tiled=True)
    queries = jnp.einsum(
        "td,hd->th",
        token_local,
        lax.all_gather(server_q, "blk", axis=1, tiled=True),
        preferred_element_type=jnp.float32,
    )
    queries = queries.astype(jnp.bfloat16)
    head_count = head_width // HD
    query_heads = queries.reshape(own_rows, head_count, HD)
    length = prompt_len[0]
    row_pages = page_table[0]
    live_slots = jnp.arange(row_pages.shape[0], dtype=jnp.int32) < page_count[0]
    row_index = jnp.arange(own_rows, dtype=jnp.int32)
    own_mask = (row_index[None, :] <= row_index[:, None]) & (row_index[None, :] < length)
    softmax_state = (
        jnp.full((head_count, own_rows), -1e30, jnp.float32),
        jnp.zeros((head_count, own_rows), jnp.float32),
        jnp.zeros((head_count, own_rows, HD), jnp.float32),
    )
    softmax_state = attend_block(
        softmax_state,
        query_heads,
        prompt_kv[0].reshape(own_rows, head_count, HD),
        prompt_kv[1].reshape(own_rows, head_count, HD),
        own_mask,
    )
    shard_piece = lax.all_gather(kv_pool, "blk", axis=1, tiled=True)
    key_count = shard_piece.shape[1]
    page_ids = jnp.arange(key_count, dtype=jnp.int32) // PAGE
    page_used = jnp.any((row_pages[None, :] == page_ids[:, None]) & live_slots[None, :], axis=1)
    key_mask = jnp.broadcast_to(page_used[None, :], (own_rows, key_count))
    running_max, row_total, weighted = attend_block(
        softmax_state,
        query_heads,
        shard_piece[0].reshape(key_count, head_count, HD),
        shard_piece[1].reshape(key_count, head_count, HD),
        key_mask,
    )
    mixed = weighted / row_total[:, :, None]
    mixed = jnp.where((row_index < length)[None, :, None], mixed, 0.0)
    mixed = jnp.transpose(mixed, (1, 0, 2)).reshape(own_rows, head_width).astype(jnp.bfloat16)
    return (server_q, mixed)


def pairs(move):
    def number(pair, core, blk, mp):
        return ((pair * 2 + core) * 2 + blk) * 4 + mp

    found = []
    for pair in range(2):
        for core in range(2):
            for blk in range(2):
                for mp in range(4):
                    target = move(pair, core, blk, mp)
                    if target is not None:
                        found.append((number(pair, core, blk, mp), number(*target)))
    return found


RING = {(0, 0): (1, 0), (1, 0): (1, 1), (1, 1): (0, 1), (0, 1): (0, 0)}
RING_MOVE = pairs(lambda p, c, b, m: (RING[p, b][0], c, RING[p, b][1], m))
CROSS_MOVE = pairs(lambda p, c, b, m: (p, c, b, m) if p == b else (b, c, p, m))
CORE_MOVE = pairs(lambda p, c, b, m: (p, 1 - c, b, m))
BLK_MOVE = pairs(lambda p, c, b, m: (p, c, 1 - b, m))
PAIR_MOVE = pairs(lambda p, c, b, m: (p, c, b, m ^ 1))
MID_MOVE = pairs(lambda p, c, b, m: (p, c, b, 3 - m) if m in (1, 2) else None)
END_MOVE = pairs(lambda p, c, b, m: (p, c, b, m ^ 1) if m in (1, 2) else None)


def cut_kernel(piece, *parts):
    half = piece.shape[0] // 2
    row = 0
    for part in parts:
        rows = part.shape[0] // 2
        for request in range(2):
            part[request * rows : (request + 1) * rows] = piece[
                request * half + row : request * half + row + rows
            ]
        row += rows


def cut(piece, first):
    rows, depth = piece.shape
    vmem = pl.BlockSpec(memory_space=pltpu.VMEM)
    return pl.pallas_call(
        cut_kernel,
        out_shape=(
            pltpu.VMEM((2 * first, depth), piece.dtype),
            pltpu.VMEM((rows - 2 * first, depth), piece.dtype),
        ),
        in_specs=[vmem],
        out_specs=(vmem, vmem),
        compiler_params=pltpu.CompilerParams(vmem_limit_bytes=8 * 1024 * 1024),
        cost_estimate=pl.CostEstimate(
            flops=0, bytes_accessed=4 * rows * depth, transcendentals=0
        ),
    )(piece)


def query_kernel(facts, *refs):
    wide = refs[:4]
    sides = (refs[4 : 4 + 2 * W_PARTS], refs[4 + 2 * W_PARTS : 4 + 4 * W_PARTS])
    total, last_w, server_q, held_t, held_w, got_t, got_w, put_w = refs[4 + 4 * W_PARTS + 1 :]
    middle, ring_half = facts[1], facts[2]
    rows, depth = sides[0][0].shape[0], held_w.shape[2]

    def fetch_t(k, source):
        return pltpu.make_async_copy(wide[k + source], held_t.at[k], got_t.at[k])

    def fetch_w(k, side, source):
        part = ring_half if source < W_PARTS else 1 - ring_half
        first_row = (part * W_PARTS + source % W_PARTS) * rows
        return pltpu.make_async_copy(
            sides[side][source].at[
                :, pl.ds(pl.multiple_of(facts[5 + 3 * k] * depth, 128), depth)
            ],
            held_w.at[k, pl.ds(pl.multiple_of(first_row, 16), rows)],
            got_w.at[k, source],
        )

    def store_w(k):
        return pltpu.make_async_copy(
            held_w.at[k],
            server_q.at[:, pl.ds(pl.multiple_of(facts[3 + 3 * k] * depth, 128), depth)],
            put_w.at[k],
        )

    for k in range(4):
        for side in range(2):

            @pl.when(facts[4 + 3 * k] == side)
            def _(k=k, side=side):
                for source in range(2 * W_PARTS):
                    fetch_w(k, side, source).start()

        if k < 2:
            fetch_t(k, 0).start()
        elif k == 2:
            for source in range(2):

                @pl.when(middle == 1 - source)
                def _(k=k, source=source):
                    fetch_t(k, source).start()

    for k in range(4):
        for source in range(2 * W_PARTS):
            fetch_w(k, 0, source).wait()
        store_w(k).start()
        if k == 3:
            last_w[...] = held_w[k]
        else:
            fetch_t(k, 0).wait()
            part = lax.dot_general(held_t[k], held_w[k], NT, preferred_element_type=F32)
            if k == 0:
                total[...] = part
            else:
                total[...] += part
    for k in range(4):
        store_w(k).wait()


def query_part(facts, wide, sides, token):
    rows, depth = wide[0].shape
    heads = 2 * W_PARTS * sides[0].shape[0]
    in_hbm = functools.partial(pltpu.with_memory_space_constraint, memory_space=pltpu.HBM)
    wide = [in_hbm(piece) for piece in wide]
    sides = [in_hbm(piece) for piece in sides]
    vmem = pl.BlockSpec(memory_space=pltpu.VMEM)
    anywhere = pl.BlockSpec(memory_space=pl.ANY)
    return pl.pallas_call(
        query_kernel,
        out_shape=(
            pltpu.VMEM((rows, heads), F32),
            pltpu.VMEM((heads, depth), BF16),
            jax.ShapeDtypeStruct((heads, 4 * depth), BF16),
        ),
        in_specs=[pl.BlockSpec(memory_space=pltpu.SMEM)] + [anywhere] * (4 + 4 * W_PARTS + 1),
        out_specs=(vmem, vmem, anywhere),
        scratch_shapes=[
            pltpu.VMEM((3, rows, depth), BF16),
            pltpu.VMEM((4, heads, depth), BF16),
            pltpu.SemaphoreType.DMA((3,)),
            pltpu.SemaphoreType.DMA((4, 2 * W_PARTS)),
            pltpu.SemaphoreType.DMA((4,)),
        ],
        compiler_params=pltpu.CompilerParams(vmem_limit_bytes=14 * 1024 * 1024),
        cost_estimate=pl.CostEstimate(
            flops=2 * 3 * rows * depth * heads,
            bytes_accessed=2 * 4 * (rows + 2 * heads) * depth,
            transcendentals=0,
        ),
    )(facts, *wide, *sides, *token)


def last_kernel(first_row, facts, mid_piece, end_piece, so_far, weights, own, send):
    middle, blk = facts[1], facts[0]
    half = own.shape[0]
    piece = jnp.where(middle == 1, mid_piece[...], end_piece[...])
    part = lax.dot_general(piece, weights[...], NT, preferred_element_type=F32)
    whole = so_far.shape[0] // 2
    upper = so_far[first_row : first_row + half] + part[:half]
    lower = so_far[whole + first_row : whole + first_row + half] + part[half:]

    @pl.when(blk == 0)
    def _():
        own[...] = upper
        send[...] = lower.astype(BF16)

    @pl.when(blk == 1)
    def _():
        own[...] = lower
        send[...] = upper.astype(BF16)


def query_last(first_row, facts, mid_piece, end_piece, so_far, weights):
    rows, depth = mid_piece.shape
    heads = weights.shape[0]
    vmem = pl.BlockSpec(memory_space=pltpu.VMEM)
    return pl.pallas_call(
        functools.partial(last_kernel, first_row),
        out_shape=(
            jax.ShapeDtypeStruct((rows // 2, heads), F32),
            jax.ShapeDtypeStruct((rows // 2, heads), BF16),
        ),
        in_specs=[pl.BlockSpec(memory_space=pltpu.SMEM)] + [vmem] * 4,
        out_specs=(vmem,) * 2,
        compiler_params=pltpu.CompilerParams(vmem_limit_bytes=6 * 1024 * 1024),
        cost_estimate=pl.CostEstimate(
            flops=2 * rows * depth * heads,
            bytes_accessed=2 * (2 * rows + heads) * depth,
            transcendentals=0,
        ),
    )(facts, mid_piece, end_piece, so_far, weights)


def window(head, width):
    low = head * HD // 128 * 128
    high = min(width, -(-(head + 1) * HD // 128) * 128)
    return low, high, head * HD - low


def to_front(wide, offset):
    if offset:
        wide = pltpu.roll(wide, wide.shape[1] - offset, 1)
    return wide[:, :256]


def align_kernel(prompt, pool_own, pool_other, out):
    width = prompt.shape[2]
    for kind in range(2):
        row = 0
        for ref in (pool_own, pool_other, prompt):
            rows = ref.shape[1]
            for head in range(width // HD):
                low, high, offset = window(head, width)
                wide = ref[kind, :, low:high].astype(F32)
                out[kind, head, row : row + rows] = to_front(wide, offset).astype(BF16)
            row += rows


def align(prompt, pool_own, pool_other):
    width = prompt.shape[2]
    keys = prompt.shape[1] + pool_own.shape[1] + pool_other.shape[1]
    vmem = pl.BlockSpec(memory_space=pltpu.VMEM)
    return pl.pallas_call(
        align_kernel,
        out_shape=jax.ShapeDtypeStruct((2, width // HD, keys, 256), BF16),
        in_specs=[vmem] * 3,
        out_specs=vmem,
        compiler_params=pltpu.CompilerParams(vmem_limit_bytes=12 * 1024 * 1024),
        cost_estimate=pl.CostEstimate(
            flops=0, bytes_accessed=8 * keys * width, transcendentals=0
        ),
    )(prompt, pool_own, pool_other)


def attend_kernel(first_row, pool_keys, facts, own_q, other_q, aligned, *refs):
    out, done, sem = refs[-3:]
    rows, width = done.shape
    heads = width // HD
    length, page_total, blk = facts[15], facts[16], facts[0]
    query = (own_q[...] + other_q[...].astype(F32)).astype(BF16).astype(F32)

    keys = 2 * pool_keys + first_row + rows
    key_at = lax.broadcasted_iota(jnp.int32, (1, keys), 1)
    own_side = key_at < pool_keys
    pages_here = pool_keys // PAGE
    page = jnp.where(own_side, blk, -blk) * pages_here + key_at // PAGE
    used = jnp.zeros((1, keys), jnp.int32)
    for slot in range(facts.shape[0] - 17):
        used = jnp.where((page == facts[17 + slot]) & (slot < page_total), 1, used)
    prompt_at = key_at - 2 * pool_keys
    seen_from = jnp.where(
        prompt_at >= 0,
        jnp.where(prompt_at < length, prompt_at, first_row + rows),
        jnp.where(used > 0, 0, first_row + rows),
    )
    row_at = first_row + lax.broadcasted_iota(jnp.int32, (rows, 1), 0)
    seen = seen_from <= row_at
    live = row_at < length
    lanes = lax.broadcasted_iota(jnp.int32, (1, 256), 1)

    raw = []
    for head in range(heads):
        low, high, offset = window(head, width)
        head_q = jnp.where(lanes < HD, to_front(query[:, low:high], offset), 0.0).astype(BF16)
        raw.append(
            lax.dot_general(head_q, aligned[0, head, :keys], NT, preferred_element_type=F32)
        )
    tiles = [None] * (width // 128)
    early = 2 * HD // 128 * 128
    copies = [
        pltpu.make_async_copy(
            done.at[:, low:high], out.at[pl.ds(first_row, rows), low:high], sem.at[at]
        )
        for at, (low, high) in enumerate(((0, early), (early, width)))
    ]

    def leave(copy, first, last):
        for tile in range(first, last):
            done[:, tile * 128 : (tile + 1) * 128] = tiles[tile].astype(BF16)
        copy.start()

    for head in range(heads):
        low, high, offset = window(head, width)
        scores = jnp.where(seen, raw[head] * HD**-0.5, -1e30)
        weights = jnp.exp(scores - jnp.max(scores, axis=1, keepdims=True))
        total = jnp.sum(weights, axis=1, keepdims=True)
        value = jnp.dot(
            weights.astype(BF16), aligned[1, head, :keys], preferred_element_type=F32
        )
        value = jnp.where(live, value * (1.0 / total), 0.0)
        if high - low > 256:
            value = jnp.concatenate([value, jnp.zeros((rows, high - low - 256), F32)], axis=1)
        if offset:
            value = pltpu.roll(value, offset, 1)
        for tile in range(low // 128, high // 128):
            part = value[:, tile * 128 - low : (tile + 1) * 128 - low]
            if tiles[tile] is None:
                tiles[tile] = part
            else:
                tiles[tile] = jnp.where(
                    lanes[:, :128] < head * HD - tile * 128, tiles[tile], part
                )
        if head == 1:
            leave(copies[0], 0, early // 128)
    leave(copies[1], early // 128, len(tiles))
    for copy in copies:
        copy.wait()


def attend(first_row, pool_keys, facts, own_q, other_q, aligned, before=None):
    rows, width = own_q.shape
    all_rows = aligned.shape[2] - 2 * pool_keys
    smem = pl.BlockSpec(memory_space=pltpu.SMEM)
    vmem = pl.BlockSpec(memory_space=pltpu.VMEM)
    in_specs = [smem] + [vmem] * 3
    operands = [facts, own_q, other_q, aligned]
    if before is not None:
        in_specs.append(pl.BlockSpec(memory_space=pl.ANY))
        operands.append(before)
    return pl.pallas_call(
        functools.partial(attend_kernel, first_row, pool_keys),
        out_shape=jax.ShapeDtypeStruct((all_rows, width), BF16),
        in_specs=in_specs,
        out_specs=pl.BlockSpec(memory_space=pl.ANY),
        scratch_shapes=[
            pltpu.VMEM((rows, width), BF16),
            pltpu.SemaphoreType.DMA((2,)),
        ],
        input_output_aliases={} if before is None else {4: 0},
        compiler_params=pltpu.CompilerParams(vmem_limit_bytes=8 * 1024 * 1024),
        cost_estimate=pl.CostEstimate(
            flops=4 * rows * 512 * width, bytes_accessed=8 * 512 * width, transcendentals=rows * 2048
        ),
    )(*operands)


def square_body(tokens, trainer_q, kv_pool, prompt_kv, page_table, page_count, prompt_len):
    dp, blk, mp = (lax.axis_index(name) for name in AXES)
    core, ring_half = dp % 2, 1 - dp // 2
    send = functools.partial(lax.ppermute, axis_name=AXES)

    near = send(tokens, perm=PAIR_MOVE)
    mid_own = send(tokens, perm=MID_MOVE)
    end_own = send(mid_own, perm=END_MOVE)
    parts = cut(near, CUT)
    mid_near = [send(parts[0], perm=MID_MOVE)]
    mid_near.append(send(parts[1], perm=MID_MOVE))
    end_near = [send(piece, perm=END_MOVE) for piece in mid_near]

    token = []
    late = []
    piece = mid_near[0][:192]
    for _ in range(1):
        piece = send(piece, perm=CORE_MOVE)
    token.append(piece)
    rows = trainer_q.shape[0] // W_PARTS
    own_w = [trainer_q[p * rows : (p + 1) * rows].astype(BF16) for p in range(W_PARTS)]
    ring = [send(piece, perm=RING_MOVE) for piece in own_w]
    cross = [send(piece, perm=CROSS_MOVE) for piece in own_w]
    ring, cross, token, _ = lax.optimization_barrier((ring, cross, token, (end_own, mid_near[0], mid_near[1], )))
    pool = kv_pool
    pool, _ = lax.optimization_barrier((kv_pool, (ring,)))
    ring_other = [send(piece, perm=CORE_MOVE) for piece in ring]
    cross_other = [send(piece, perm=CORE_MOVE) for piece in cross]
    pool_other = send(pool, perm=BLK_MOVE)

    third = jnp.where(mp < 2, 2, 1)
    last = jnp.where(mp < 2, 3, 0)
    middle = (mp == 1) | (mp == 2)
    facts = [blk, middle, ring_half]
    for place_at in (mp, mp ^ 1, third, last):
        facts += [place_at, place_at // 2 != core, place_at % 2]
    facts += [prompt_len[0], page_count[0]]
    facts = jnp.stack([jnp.asarray(f, jnp.int32) for f in facts])
    facts = jnp.concatenate([facts, page_table[0]])
    so_far, last_w, server_q = query_part(
        facts, (tokens, near, mid_own, end_own), (*ring, *cross, *ring_other, *cross_other), token + late
    )
    own_q, send_q = zip(
        *(query_last(c * CUT, facts, mid_near[c], end_near[c], so_far, last_w) for c in range(2))
    )
    other_q = [send(piece, perm=BLK_MOVE) for piece in send_q]

    aligned = align(prompt_kv, kv_pool, pool_other)
    out = None
    for c in range(2):
        out = attend(
            c * CUT,
            kv_pool.shape[1],
            facts,
            own_q[c],
            other_q[c],
            aligned,
            out,
        )
    return (server_q, out)


def solution(mesh):
    in_specs = (
        P("dp", ("blk", "mp")),
        P(("mp", "blk"), "dp"),
        P(None, ("dp", "blk"), "mp"),
        P(None, ("dp", "blk"), "mp"),
        P(("dp", "blk"), None),
        P(("dp", "blk")),
        P(("dp", "blk")),
    )
    out_specs = (P("mp", "blk"), P(("dp", "blk"), "mp"))
    square = dict(mesh.shape) == {"dp": 4, "blk": 2, "mp": 4}
    return jax.shard_map(
        square_body if square else body,
        mesh=mesh,
        in_specs=in_specs,
        out_specs=out_specs,
        check_vma=False,
    )
```
